32 devices in a mesh: seq: 8 (over z, y), head: 4 (over x, core).
Axes of the slice: x: 2, y: 2, z: 4, core: 2. Of those that a mesh axis runs over, the one named last changes fastest.
Arguments:
- queries: bfloat16 [8192, 1024], P('seq', 'head'), may hold values from -6 to 6
- key_rows: bfloat16 [8192, 1024], P('seq', 'head'), may hold values from -6 to 6
- value_rows: bfloat16 [8192, 1024], P('seq', 'head'), may hold values from -6 to 6
- attn_out: bfloat16 [8192, 1024], P('seq', 'head'), may hold values from -6 to 6
- gate_pre: bfloat16 [8192, 1024], P('seq', 'head'), may hold values from -6 to 6
- out_grad: bfloat16 [8192, 1024], P('seq', 'head'), may hold values from -6 to 6
- segments: int32 [8192], P('seq'), may hold values from 0 to 1, never falling along the last dimension, each value on 1 to 6145 neighbouring positions
- projections: bfloat16 [4, 1024, 1024], P(None, None, 'head'), may hold values from -0.1875 to 0.1875
Outputs:
- input_grad: bfloat16 [8192, 1024], P('seq', 'head')
The draws below stay inside these ranges and needn't reach their ends.
Inputs may be any that keep to these rules, and one draw needn't show every extreme that they name: `segments`: each user's rows are contiguous and ordered; a user has 1 to 6145 rows and one user has exactly 6145, so no user spans more than 6 + 1 = 7 shards of 1024 rows.
All inputs are finite; a program needn't handle non-finite values.
Results may differ from the reference program's by a relative error of at most 0.0064.
Values may be sent and summed in bfloat16 or wider, within the bound.
A program may use at most 128 MiB of HBM per device.

```python
import math
import jax
import jax.numpy as jnp
import numpy as np
from jax import lax

D = 1024
HEAD_DIM = 128
WINDOW = 6
ROWS = 1024
TOKENS = 8192
USERS = 2
N_SEQ = 8


def shard_levels(rng, extent, pieces, low, high):
    loudness, own = 1.0, jax.random.fold_in(rng, 6)
    for axis_at, parts in pieces:
        draws = jnp.exp(jax.random.uniform(jax.random.fold_in(own, axis_at), (parts,), jnp.float32, low / len(pieces), high / len(pieces)))
        loudness = loudness * jnp.repeat(draws, extent[axis_at] // parts).reshape([-1 if axis == axis_at else 1 for axis in range(len(extent))])
    return loudness


def split_up(count, total, reach, skew):
    weights = [(1 << 20) // math.isqrt(grade ** skew) + 1 for grade in range(2, count + 1)]
    rest, given = total - reach - (count - 1), [1] * (count - 1)
    while rest > 0:
        candidates = [i for i in range(count - 1) if given[i] < reach]
        mass, left = sum([weights[i] for i in candidates]), rest
        for i in candidates:
            addition = min(reach - given[i], max(1, left * weights[i] // mass), rest)
            given[i] = given[i] + addition
            rest = rest - addition
    return np.array([reach] + given)


def uneven(key, count, total, bound, lean):
    if count == 2:
        one = jax.random.randint(key, (), max(1, total - bound), min(bound, total - 1) + 1)
        return jnp.stack([one, total - one])
    lengths = jnp.asarray(split_up(count, total, bound, lean), jnp.int32)
    couples = (count - 1) // 2
    donor, receiver = lengths[1:1 + 2 * couples:2], lengths[2:2 + 2 * couples:2]
    slack = jnp.minimum(donor - 1, bound - receiver)
    shifted = jax.random.randint(jax.random.fold_in(key, 1), (couples,), 0, 1 << 20) % (slack + 1)
    lengths = lengths.at[1:1 + 2 * couples:2].set(donor - shifted).at[2:2 + 2 * couples:2].set(receiver + shifted)
    return lengths[jax.random.permutation(jax.random.fold_in(key, 2), count)]


def noise(own_key, extent, spread, most, split=(), kind=jnp.bfloat16):
    drawn = jax.random.normal(own_key, extent, jnp.float32) * spread
    if len(split) > 0:
        drawn = shard_levels(own_key, extent, split, -0.22, 0.18) * drawn
    return jnp.clip(drawn, min=-most, max=most).astype(kind)


def setup_inputs(seed: int = 0) -> dict:
    seeds = jax.random.split(jax.random.key(seed), 9)
    return {
        "queries": noise(seeds[0], (TOKENS, D), 1.0, 6.0, ((0, 8), (1, 4))),
        "key_rows": noise(seeds[1], (TOKENS, D), 1.0, 6.0, ((0, 8), (1, 4))),
        "value_rows": noise(seeds[2], (TOKENS, D), 1.0, 6.0, ((0, 8), (1, 4))),
        "attn_out": noise(seeds[3], (TOKENS, D), 1.0, 6.0, ((0, 8), (1, 4))),
        "gate_pre": noise(seeds[4], (TOKENS, D), 1.0, 6.0, ((0, 8), (1, 4))),
        "out_grad": noise(seeds[5], (TOKENS, D), 1.0, 6.0, ((0, 8), (1, 4))),
        "segments": jnp.searchsorted(jnp.cumsum(uneven(seeds[6], USERS, TOKENS, 6 * ROWS + 1, 0)), jnp.arange(TOKENS), side="right").astype(jnp.int32),
        "projections": noise(seeds[7], (4, D, D), D ** -0.5, 0.1875, ((2, 4),)),
    }


def silu_slope(values_in):
    sigma = jax.nn.sigmoid(values_in)
    return sigma * (1.0 + values_in * (1.0 - sigma))

def rounded(values_in):
    return lax.optimization_barrier(values_in.astype(jnp.bfloat16)).astype(jnp.float32)

def norm_backward(attn_out, gate_pre, out_grad):
    row_count, width = attn_out.shape
    head_count = width // HEAD_DIM
    saved = attn_out.astype(jnp.float32).reshape(row_count, head_count, HEAD_DIM)
    centred = saved - lax.optimization_barrier(jnp.mean(saved, axis=-1, keepdims=True))
    inverse = lax.rsqrt(lax.optimization_barrier(jnp.mean(centred * centred, axis=-1, keepdims=True)) + 1e-06)
    normed = centred * inverse
    gate_in = gate_pre.astype(jnp.float32)
    grad_in = out_grad.astype(jnp.float32)
    gate_grad = grad_in * normed.reshape(row_count, width) * silu_slope(gate_in)
    normed_grad = (grad_in * jax.nn.silu(gate_in)).reshape(row_count, head_count, HEAD_DIM)
    attn_grad = inverse * (normed_grad - lax.optimization_barrier(jnp.mean(normed_grad, axis=-1, keepdims=True)) - normed * lax.optimization_barrier(jnp.mean(normed_grad * normed, axis=-1, keepdims=True)))
    return (attn_grad.reshape(row_count, width).astype(jnp.bfloat16), gate_grad.astype(jnp.bfloat16))

def reference(queries, key_rows, value_rows, attn_out, gate_pre, out_grad, segments, projections):
    attn_grad, gate_grad = norm_backward(attn_out, gate_pre, out_grad)
    head_count = D // HEAD_DIM
    scale = HEAD_DIM ** (-0.5)
    causal = jnp.arange(ROWS)[:, None] >= jnp.arange(ROWS)[None, :]

    def take(source, start):
        return lax.dynamic_slice_in_dim(source, start, ROWS, 0)

    def split_heads(source):
        return source.astype(jnp.float32).reshape(ROWS, head_count, HEAD_DIM)

    def per_shard(carry, shard):
        key_acc, value_acc = carry
        start = (shard * ROWS).astype(jnp.int32)
        query_blk = split_heads(take(queries, start))
        grad_blk = split_heads(take(attn_grad, start))
        owner_q = take(segments, start)
        query_acc = jnp.zeros((ROWS, head_count, HEAD_DIM), jnp.float32)
        for distance in range(WINDOW + 1):
            source_shard = jnp.maximum(shard - distance, 0).astype(jnp.int32)
            key_start = (source_shard * ROWS).astype(jnp.int32)
            key_blk = split_heads(take(key_rows, key_start))
            value_blk = split_heads(take(value_rows, key_start))
            owner_k = take(segments, key_start)
            allowed = (owner_q[:, None] == owner_k[None, :]) & (shard - distance >= 0)
            if distance == 0:
                allowed = allowed & causal
            scores = jnp.einsum('qhd,khd->hqk', query_blk, key_blk) * scale
            weights = rounded(jnp.where(allowed, jax.nn.silu(scores), 0.0))
            slope_in = jnp.einsum('qhd,khd->hqk', grad_blk, value_blk)
            score_grad = rounded(jnp.where(allowed, slope_in * silu_slope(scores) * scale, 0.0))
            query_acc = query_acc + jnp.einsum('hqk,khd->qhd', score_grad, key_blk)
            key_add = jnp.einsum('hqk,qhd->khd', score_grad, query_blk).reshape(ROWS, D)
            value_add = jnp.einsum('hqk,qhd->khd', weights, grad_blk).reshape(ROWS, D)
            key_acc = lax.dynamic_update_slice_in_dim(key_acc, take(key_acc, key_start) + key_add, key_start, 0)
            value_acc = lax.dynamic_update_slice_in_dim(value_acc, take(value_acc, key_start) + value_add, key_start, 0)
        return ((key_acc, value_acc), query_acc.reshape(ROWS, D))
    zero_grads = jnp.zeros((TOKENS, D), jnp.float32)
    (key_acc, value_acc), query_parts = lax.scan(per_shard, (zero_grads, zero_grads), jnp.arange(N_SEQ, dtype=jnp.int32))
    query_acc = query_parts.reshape(TOKENS, D)
    stacked = jnp.stack([query_acc.astype(jnp.bfloat16), key_acc.astype(jnp.bfloat16), value_acc.astype(jnp.bfloat16), gate_grad])
    result = jnp.einsum('prh,pdh->rd', stacked.astype(jnp.float32), projections.astype(jnp.float32))
    return result.astype(jnp.bfloat16)
```

```python
import functools

import jax
import jax.numpy as jnp
from jax import lax
from jax.experimental import pallas as pl
from jax.experimental.pallas import tpu as pltpu
from jax.sharding import PartitionSpec as P

HEAD_DIM = 128
WINDOW = 6
PAIR = 2
TILE = 512
SCALE = HEAD_DIM ** (-0.5)
BF16 = jnp.bfloat16
F32 = jnp.float32


def dot(left, right, dims):
    return lax.dot_general(left, right, (dims, ((), ())), preferred_element_type=F32)


def prepare_kernel(
    place, queries, keys, values, attn_out, gate_pre, out_grad,
    query_own, query_other, key_own, key_other, gate_grad,
):
    lane = place[0]
    for slot, (to_query, to_key) in enumerate(((query_own, key_own), (query_other, key_other))):
        head = lane if slot == 0 else 1 - lane
        cols = pl.ds(pl.multiple_of(head * HEAD_DIM, HEAD_DIM), HEAD_DIM)
        to_query[0] = queries[:, cols]
        to_key[0] = keys[:, cols]
        to_key[1] = values[:, cols]
        saved = attn_out[:, cols].astype(F32)
        centred = saved - jnp.mean(saved, axis=-1, keepdims=True)
        inverse = lax.rsqrt(jnp.mean(centred * centred, axis=-1, keepdims=True) + 1e-06)
        normed = centred * inverse
        gate_in = gate_pre[:, cols].astype(F32)
        grad_in = out_grad[:, cols].astype(F32)
        sigma = jax.nn.sigmoid(gate_in)
        gate_grad[:, cols] = (
            grad_in * normed * (sigma * (1.0 + gate_in * (1.0 - sigma)))
        ).astype(BF16)
        normed_grad = grad_in * (gate_in * sigma)
        to_query[1] = (
            inverse
            * (
                normed_grad
                - jnp.mean(normed_grad, axis=-1, keepdims=True)
                - normed * jnp.mean(normed_grad * normed, axis=-1, keepdims=True)
            )
        ).astype(BF16)


def prepare(lane, queries, keys, values, attn_out, gate_pre, out_grad):
    rows, width = queries.shape
    step = min(rows, 256)
    wide = pl.BlockSpec((step, width), lambda i, place: (i, 0))
    pair = pl.BlockSpec((2, step, HEAD_DIM), lambda i, place: (0, i, 0))
    pair_shape = jax.ShapeDtypeStruct((2, rows, HEAD_DIM), BF16)
    return pl.pallas_call(
        prepare_kernel,
        grid_spec=pltpu.PrefetchScalarGridSpec(
            num_scalar_prefetch=1,
            grid=(rows // step,),
            in_specs=[wide] * 6,
            out_specs=[pair] * 4 + [wide],
        ),
        out_shape=[pair_shape] * 4 + [jax.ShapeDtypeStruct((rows, width), BF16)],
        compiler_params=pltpu.CompilerParams(vmem_limit_bytes=32 * 2**20),
        cost_estimate=pl.CostEstimate(
            flops=40 * rows * width, bytes_accessed=22 * rows * width, transcendentals=rows * width
        ),
        name="prepare",
    )(lane, queries, keys, values, attn_out, gate_pre, out_grad)


def attend_kernel(first, last, ids, segs, seg_rows, *refs):
    refs = list(refs)
    sources = [refs.pop(0) for _ in range(4 if first else 6)]
    query_out, own_out, other_out, query_in, key_in, key_acc, query_acc, sems = refs
    rows = query_in.shape[2]
    per = rows // TILE
    count = 2 * per

    targets = [query_in.at[0], query_in.at[1], key_in.at[0], key_in.at[1]]
    if not first:
        targets += [key_acc.at[0], key_acc.at[1]]
    copies = [
        pltpu.make_async_copy(source, target, sems.at[n])
        for n, (source, target) in enumerate(zip(sources, targets))
    ]
    for copy in copies:
        copy.start()
    query_acc[...] = jnp.zeros_like(query_acc)
    if first:
        key_acc[...] = jnp.zeros_like(key_acc)
    for copy in copies:
        copy.wait()

    def body(index, carry):
        q_idx, k_idx = index // count, index % count
        q_blk, k_blk = q_idx // per, k_idx // per
        q_off = pl.multiple_of((q_idx % per) * TILE, TILE)
        k_off = pl.multiple_of((k_idx % per) * TILE, TILE)
        q_shard, k_shard = ids[q_blk], ids[2 + k_blk]
        q_first, k_first = q_shard * rows + q_off, k_shard * rows + k_off
        q_last, k_last = q_first + TILE - 1, k_first + TILE - 1
        live = (ids[4] > 0) & (k_first <= q_last) & (segs[k_last] >= segs[q_first])
        full = (k_last <= q_first) & (segs[k_first] == segs[q_last])
        q_rows, k_rows = pl.ds(q_off, TILE), pl.ds(k_off, TILE)

        def work(masked):
            query = query_in[q_blk, 0, q_rows, :]
            grad = query_in[q_blk, 1, q_rows, :]
            key = key_in[k_blk, 0, k_rows, :]
            value = key_in[k_blk, 1, k_rows, :]
            half = dot(key, query, ((1,), (1,))) * (SCALE / 2)
            slope_in = dot(value, grad, ((1,), (1,)))
            tanh = jnp.tanh(half)
            upper = 1.0 + tanh
            weights = half * upper
            score_grad = slope_in * (upper + weights * (1.0 - tanh))
            if masked:
                seg_q = seg_rows[pl.ds(q_shard, 1), q_rows]
                seg_k = seg_rows[pl.ds(k_shard, 1), k_rows]
                seg_k = jnp.transpose(jnp.broadcast_to(seg_k, (HEAD_DIM, TILE)))[:, :1]
                place_k = k_first + lax.broadcasted_iota(jnp.int32, (TILE, TILE), 0)
                place_q = q_first + lax.broadcasted_iota(jnp.int32, (TILE, TILE), 1)
                allowed = (seg_q == seg_k) & (place_k <= place_q)
                weights = jnp.where(allowed, weights, 0.0)
                score_grad = jnp.where(allowed, score_grad, 0.0)
            weights = weights.astype(BF16)
            score_grad = score_grad.astype(BF16)
            key_acc[k_blk, 0, k_rows, :] += dot(score_grad, query, ((1,), (0,)))
            key_acc[k_blk, 1, k_rows, :] += dot(weights, grad, ((1,), (0,)))
            query_acc[q_blk, q_rows, :] += dot(score_grad, key, ((0,), (0,)))

        @pl.when(live & full)
        def _():
            work(False)

        @pl.when(live & jnp.logical_not(full))
        def _():
            work(True)

        return carry

    lax.fori_loop(0, count * count, body, 0)
    query_out[...] = (query_acc[...] * (SCALE / 2)).astype(query_out.dtype)
    for blk, out in enumerate((own_out, other_out)):
        if last:
            out[0] = (key_acc[blk, 0] * (SCALE / 2)).astype(BF16)
            out[1] = key_acc[blk, 1].astype(BF16)
        else:
            out[...] = key_acc[blk]


def attend(first, last, ids, segs, seg_rows, queries, keys, acc):
    rows = queries[0].shape[1]
    any_spec = pl.BlockSpec(memory_space=pl.ANY)
    vmem = pl.BlockSpec(memory_space=pltpu.VMEM)
    acc = () if first else tuple(acc)
    acc_shape = jax.ShapeDtypeStruct((2, rows, HEAD_DIM), BF16 if last else F32)
    pairs = (2 * rows) ** 2
    return pl.pallas_call(
        functools.partial(attend_kernel, first, last),
        grid_spec=pltpu.PrefetchScalarGridSpec(
            num_scalar_prefetch=2,
            grid=(),
            in_specs=[vmem] + [any_spec] * (4 + len(acc)),
            out_specs=[vmem] * 3,
            scratch_shapes=[
                pltpu.VMEM((2, 2, rows, HEAD_DIM), BF16),
                pltpu.VMEM((2, 2, rows, HEAD_DIM), BF16),
                pltpu.VMEM((2, 2, rows, HEAD_DIM), F32),
                pltpu.VMEM((2, rows, HEAD_DIM), F32),
                pltpu.SemaphoreType.DMA((6,)),
            ],
        ),
        out_shape=[
            jax.ShapeDtypeStruct((2, rows, HEAD_DIM), F32 if first else BF16),
            acc_shape,
            acc_shape,
        ],
        compiler_params=pltpu.CompilerParams(vmem_limit_bytes=48 * 2**20),
        cost_estimate=pl.CostEstimate(
            flops=10 * pairs * HEAD_DIM, bytes_accessed=14 * rows * HEAD_DIM * 4, transcendentals=pairs
        ),
        name="attend",
    )(ids, segs, seg_rows, *queries, *keys, *acc)


def project_kernel(
    place, query_own, key_own, query_other, key_other, gate_grad, weights, out, stacked
):
    @pl.when(pl.program_id(0) == 0)
    def _():
        lane = place[0]
        own = pl.ds(pl.multiple_of(lane * HEAD_DIM, HEAD_DIM), HEAD_DIM)
        other = pl.ds(pl.multiple_of((1 - lane) * HEAD_DIM, HEAD_DIM), HEAD_DIM)
        stacked[0, :, own] = query_own[...]
        stacked[0, :, other] = query_other[...]
        for part in range(2):
            stacked[1 + part, :, own] = key_own[part]
            stacked[1 + part, :, other] = key_other[part]
        stacked[3] = gate_grad[...]

    total = dot(stacked[0], weights[0], ((1,), (1,)))
    for part in range(1, 4):
        total = total + dot(stacked[part], weights[part], ((1,), (1,)))
    out[0] = total.astype(out.dtype)


def project(place, count, grads, projections, dtype):
    gate_grad = grads[-1]
    rows, width = gate_grad.shape
    whole = lambda array: pl.BlockSpec(array.shape, lambda i, place: (0,) * array.ndim)
    return pl.pallas_call(
        project_kernel,
        grid_spec=pltpu.PrefetchScalarGridSpec(
            num_scalar_prefetch=1,
            grid=(count,),
            in_specs=[whole(grad) for grad in grads]
            + [pl.BlockSpec((4, width, width), lambda i, place: (0, place[1 + i], 0))],
            out_specs=pl.BlockSpec((1, rows, width), lambda i, place: (i, 0, 0)),
            scratch_shapes=[pltpu.VMEM((4, rows, width), BF16)],
        ),
        out_shape=jax.ShapeDtypeStruct((count, rows, width), dtype),
        compiler_params=pltpu.CompilerParams(vmem_limit_bytes=40 * 2**20),
        cost_estimate=pl.CostEstimate(
            flops=8 * count * rows * width * width,
            bytes_accessed=rows * width * (8 + 4 * count),
            transcendentals=0,
        ),
        name="project",
    )(place, *grads, projections)


def per_device(queries, key_rows, value_rows, attn_out, gate_pre, out_grad, segments, projections):
    rows = queries.shape[0]
    shards, groups = lax.axis_size("seq"), lax.axis_size("head")
    shard, group = lax.axis_index("seq"), lax.axis_index("head")
    pairs = shards // PAIR
    pair, lane = shard // PAIR, shard % PAIR

    def swap(block):
        return lax.ppermute(block, "seq", [(i, i ^ 1) for i in range(shards)])

    def shift(block, distance):
        return lax.ppermute(
            block,
            "seq",
            [(i, i + PAIR * distance) for i in range(shards) if 0 <= i + PAIR * distance < shards],
        )

    segs = lax.all_gather(segments, "seq", tiled=True)
    seg_rows = segs.astype(F32).reshape(shards, rows)
    lane_arg = jnp.reshape(lane, (1,)).astype(jnp.int32)
    query_own, query_other, key_own, key_other, gate_grad = prepare(
        lane_arg, queries, key_rows, value_rows, attn_out, gate_pre, out_grad
    )
    block_a, block_b = query_own, swap(query_other)
    keys = (key_own, swap(key_other))

    reach = min((WINDOW + 1) // PAIR, pairs - 1)
    acc, query_sum = None, None
    for distance in range(reach + 1):
        if distance > 0:
            block_a, block_b = shift(block_a, -1), shift(block_b, -1)
        far = PAIR * jnp.minimum(pair + distance, pairs - 1)
        ids = jnp.stack(
            [far + lane, far + 1 - lane, shard, shard ^ 1, (pair + distance < pairs)]
        ).astype(jnp.int32)
        part, acc_own, acc_other = attend(
            distance == 0, distance == reach, ids, segs, seg_rows, (block_a, block_b), keys, acc
        )
        acc = (acc_own, acc_other)
        if distance == 0:
            query_sum = part
        else:
            query_sum = query_sum + shift(part, distance).astype(F32)
    query_sum = query_sum.astype(BF16)
    acc_other = swap(acc[1])
    query_other = swap(query_sum[1])
    grads = (query_sum[0], acc[0], query_other, acc_other, gate_grad)

    def blocks_of(targets):
        return jnp.stack([lane] + targets).astype(jnp.int32)

    bits = []
    while (1 << len(bits)) < groups:
        bits.append(1 << len(bits))
    kept = list(range(groups))

    def across(block, bit):
        return lax.ppermute(block, "head", [(i, i ^ bit) for i in range(groups)])

    near = [offset for offset in kept if offset & 1 == 0]
    sent = [offset for offset in kept if offset & 1 == 1]
    away = project(blocks_of([group ^ o for o in sent]), len(sent), grads, projections, BF16)
    arrived = across(away, 1)
    total = project(blocks_of([group ^ o for o in near]), len(near), grads, projections, F32)
    total = total + arrived.astype(F32)
    for bit in bits[1:]:
        sent = [n for n, offset in enumerate(near) if offset & bit]
        held = [n for n, offset in enumerate(near) if not offset & bit]
        arrived = across(jnp.stack([total[n] for n in sent]).astype(BF16), bit)
        total = jnp.stack([total[n] for n in held]) + arrived.astype(F32)
        near = [near[n] for n in held]
    return total[0].astype(BF16)


def solution(mesh):
    return jax.shard_map(
        per_device,
        mesh=mesh,
        in_specs=(
            P("seq", "head"),
            P("seq", "head"),
            P("seq", "head"),
            P("seq", "head"),
            P("seq", "head"),
            P("seq", "head"),
            P("seq"),
            P(None, None, "head"),
        ),
        out_specs=P("seq", "head"),
        check_vma=False,
    )
```

```python
import functools

import jax
import jax.numpy as jnp
from jax import lax
from jax.experimental import pallas as pl
from jax.experimental.pallas import tpu as pltpu
from jax.sharding import PartitionSpec as P

HEAD_DIM = 128
WINDOW = 6
PAIR = 2
TILE = 512
CHUNK = 256
SCALE = HEAD_DIM ** (-0.5)
VMEM_BYTES = 60 * 2**20
BF16 = jnp.bfloat16
F32 = jnp.float32


def dot(left, right, dims):
    return lax.dot_general(left, right, (dims, ((), ())), preferred_element_type=F32)


def prepare_kernel(
    shards, queries, keys, values, attn_out, gate_pre, out_grad, segments,
    query_own, query_other, key_own, key_other, gate_grad, seg_all, send_sems, recv_sems,
):
    me = lax.axis_index("seq")
    lane = lax.rem(me, PAIR)
    step = pl.program_id(0)

    def seg_copies():
        return [
            pltpu.make_async_remote_copy(
                src_ref=segments,
                dst_ref=seg_all.at[me],
                send_sem=send_sems.at[offset],
                recv_sem=recv_sems.at[offset],
                device_id={"seq": lax.rem(me + offset, shards)},
                device_id_type=pl.DeviceIdType.MESH,
            )
            for offset in range(1, shards)
        ]

    @pl.when(step == 0)
    def _():
        barrier = pltpu.get_barrier_semaphore()
        for offset in range(1, shards):
            pl.semaphore_signal(
                barrier,
                inc=1,
                device_id={"seq": lax.rem(me + offset, shards)},
                device_id_type=pl.DeviceIdType.MESH,
            )

    @pl.when(step == 1)
    def _():
        pl.semaphore_wait(pltpu.get_barrier_semaphore(), shards - 1)
        for copy in seg_copies():
            copy.start()
        own = pltpu.make_async_copy(segments, seg_all.at[me], send_sems.at[0])
        own.start()
        own.wait()

    for slot, (to_query, to_key) in enumerate(((query_own, key_own), (query_other, key_other))):
        head = lane if slot == 0 else 1 - lane
        cols = pl.ds(pl.multiple_of(head * HEAD_DIM, HEAD_DIM), HEAD_DIM)
        to_query[0] = queries[:, cols]
        to_key[0] = keys[:, cols]
        to_key[1] = values[:, cols]
        saved = attn_out[:, cols].astype(F32)
        centred = saved - jnp.mean(saved, axis=-1, keepdims=True)
        inverse = lax.rsqrt(jnp.mean(centred * centred, axis=-1, keepdims=True) + 1e-06)
        normed = centred * inverse
        gate_in = gate_pre[:, cols].astype(F32)
        grad_in = out_grad[:, cols].astype(F32)
        sigma = jax.nn.sigmoid(gate_in)
        gate_grad[:, cols] = (
            grad_in * normed * (sigma * (1.0 + gate_in * (1.0 - sigma)))
        ).astype(BF16)
        normed_grad = grad_in * (gate_in * sigma)
        to_query[1] = (
            inverse
            * (
                normed_grad
                - jnp.mean(normed_grad, axis=-1, keepdims=True)
                - normed * jnp.mean(normed_grad * normed, axis=-1, keepdims=True)
            )
        ).astype(BF16)

    @pl.when(step == pl.num_programs(0) - 1)
    def _():
        for copy in seg_copies():
            copy.wait()


def prepare(shards, queries, keys, values, attn_out, gate_pre, out_grad, segments):
    rows, width = queries.shape
    step = min(rows // 2, 256)
    wide = pl.BlockSpec((step, width), lambda i: (i, 0))
    pair = pl.BlockSpec((2, step, HEAD_DIM), lambda i: (0, i, 0))
    pair_shape = jax.ShapeDtypeStruct((2, rows, HEAD_DIM), BF16)
    any_spec = pl.BlockSpec(memory_space=pl.ANY)
    return pl.pallas_call(
        functools.partial(prepare_kernel, shards),
        grid=(rows // step,),
        in_specs=[wide] * 6 + [any_spec],
        out_specs=[pair] * 4 + [wide, any_spec],
        out_shape=[pair_shape] * 4
        + [
            jax.ShapeDtypeStruct((rows, width), BF16),
            jax.ShapeDtypeStruct((shards,) + segments.shape, segments.dtype),
        ],
        scratch_shapes=[
            pltpu.SemaphoreType.DMA((shards,)),
            pltpu.SemaphoreType.DMA((shards,)),
        ],
        compiler_params=pltpu.CompilerParams(
            vmem_limit_bytes=VMEM_BYTES, collective_id=0, has_side_effects=True
        ),
        cost_estimate=pl.CostEstimate(
            flops=40 * rows * width, bytes_accessed=22 * rows * width, transcendentals=rows * width
        ),
        name="prepare",
    )(queries, keys, values, attn_out, gate_pre, out_grad, segments)


def attend_kernel(first, last, ids, segs, seg_rows, *refs):
    refs = list(refs)
    sources = [refs.pop(0) for _ in range(4 if first else 6)]
    query_own, query_other, own_out, other_out, query_in, key_in, key_acc, query_acc, sems = refs
    rows = query_in.shape[2]
    per = rows // TILE
    count = 2 * per

    targets = [query_in.at[0], query_in.at[1], key_in.at[0], key_in.at[1]]
    if not first:
        targets += [key_acc.at[0], key_acc.at[1]]
    copies = [
        pltpu.make_async_copy(source, target, sems.at[n])
        for n, (source, target) in enumerate(zip(sources, targets))
    ]
    for copy in copies:
        copy.start()
    query_acc[...] = jnp.zeros_like(query_acc)
    if first:
        key_acc[...] = jnp.zeros_like(key_acc)
    for copy in copies:
        copy.wait()

    def body(index, carry):
        q_idx, k_idx = index // count, index % count
        q_blk, k_blk = q_idx // per, k_idx // per
        q_off = pl.multiple_of((q_idx % per) * TILE, TILE)
        k_off = pl.multiple_of((k_idx % per) * TILE, TILE)
        q_shard, k_shard = ids[q_blk], ids[2 + k_blk]
        q_first, k_first = q_shard * rows + q_off, k_shard * rows + k_off
        q_last, k_last = q_first + TILE - 1, k_first + TILE - 1
        live = (ids[4] > 0) & (k_first <= q_last) & (segs[k_last] >= segs[q_first])
        full = (k_last <= q_first) & (segs[k_first] == segs[q_last])
        q_rows = pl.ds(q_off, TILE)

        def work(masked):
            query = query_in[q_blk, 0, q_rows, :]
            grad = query_in[q_blk, 1, q_rows, :]
            if masked:
                seg_q = seg_rows[pl.ds(q_shard, 1), q_rows]
                place_q = q_first + lax.broadcasted_iota(jnp.int32, (CHUNK, TILE), 1)

            def products(chunk):
                spot = pl.ds(k_off + chunk * CHUNK, CHUNK)
                key = key_in[k_blk, 0, spot, :]
                value = key_in[k_blk, 1, spot, :]
                return (
                    spot,
                    key,
                    dot(key, query, ((1,), (1,))),
                    dot(value, grad, ((1,), (1,))),
                )

            chunks = TILE // CHUNK
            ready, query_part = products(0), None
            for chunk in range(chunks):
                spot, key, scores, slope_in = ready
                if chunk + 1 < chunks:
                    ready = products(chunk + 1)
                half = scores * (SCALE / 2)
                tanh = jnp.tanh(half)
                upper = 1.0 + tanh
                weights = half * upper
                score_grad = slope_in * (upper + weights * (1.0 - tanh))
                if masked:
                    seg_k = seg_rows[pl.ds(k_shard, 1), spot]
                    seg_k = jnp.transpose(jnp.broadcast_to(seg_k, (HEAD_DIM, CHUNK)))[:, :1]
                    place_k = (k_first + chunk * CHUNK) + lax.broadcasted_iota(
                        jnp.int32, (CHUNK, TILE), 0
                    )
                    allowed = (seg_q == seg_k) & (place_k <= place_q)
                    weights = jnp.where(allowed, weights, 0.0)
                    score_grad = jnp.where(allowed, score_grad, 0.0)
                weights = weights.astype(BF16)
                score_grad = score_grad.astype(BF16)
                key_acc[k_blk, 0, spot, :] += dot(score_grad, query, ((1,), (0,)))
                key_acc[k_blk, 1, spot, :] += dot(weights, grad, ((1,), (0,)))
                part = dot(score_grad, key, ((0,), (0,)))
                query_part = part if query_part is None else query_part + part
            query_acc[q_blk, q_rows, :] += query_part

        @pl.when(live & full)
        def _():
            work(False)

        @pl.when(live & jnp.logical_not(full))
        def _():
            work(True)

        return carry

    lax.fori_loop(0, count * count, body, 0)
    for blk, out in enumerate((query_own, query_other)):
        out[...] = (query_acc[blk] * (SCALE / 2)).astype(out.dtype)
    for blk, out in enumerate((own_out, other_out)):
        if last:
            out[0] = (key_acc[blk, 0] * (SCALE / 2)).astype(BF16)
            out[1] = key_acc[blk, 1].astype(BF16)
        else:
            out[...] = key_acc[blk]


def attend(first, last, ids, segs, seg_rows, queries, keys, acc):
    rows = queries[0].shape[1]
    any_spec = pl.BlockSpec(memory_space=pl.ANY)
    vmem = pl.BlockSpec(memory_space=pltpu.VMEM)
    acc = () if first else tuple(acc)
    acc_shape = jax.ShapeDtypeStruct((2, rows, HEAD_DIM), BF16 if last else F32)
    pairs = (2 * rows) ** 2
    return pl.pallas_call(
        functools.partial(attend_kernel, first, last),
        grid_spec=pltpu.PrefetchScalarGridSpec(
            num_scalar_prefetch=2,
            grid=(),
            in_specs=[vmem] + [any_spec] * (4 + len(acc)),
            out_specs=[vmem] * 4,
            scratch_shapes=[
                pltpu.VMEM((2, 2, rows, HEAD_DIM), BF16),
                pltpu.VMEM((2, 2, rows, HEAD_DIM), BF16),
                pltpu.VMEM((2, 2, rows, HEAD_DIM), F32),
                pltpu.VMEM((2, rows, HEAD_DIM), F32),
                pltpu.SemaphoreType.DMA((6,)),
            ],
        ),
        out_shape=[
            jax.ShapeDtypeStruct((rows, HEAD_DIM), F32 if first else BF16),
            jax.ShapeDtypeStruct((rows, HEAD_DIM), BF16),
            acc_shape,
            acc_shape,
        ],
        compiler_params=pltpu.CompilerParams(vmem_limit_bytes=VMEM_BYTES),
        cost_estimate=pl.CostEstimate(
            flops=10 * pairs * HEAD_DIM, bytes_accessed=14 * rows * HEAD_DIM * 4, transcendentals=pairs
        ),
        name="attend",
    )(ids, segs, seg_rows, *queries, *keys, *acc)


def project_early_kernel(place, key_own, key_other, gate_grad, weights, out, stacked):
    @pl.when(pl.program_id(0) == 0)
    def _():
        own = pl.ds(pl.multiple_of(place[0] * HEAD_DIM, HEAD_DIM), HEAD_DIM)
        other = pl.ds(pl.multiple_of((1 - place[0]) * HEAD_DIM, HEAD_DIM), HEAD_DIM)
        for part in range(2):
            stacked[part, :, own] = key_own[part]
            stacked[part, :, other] = key_other[part]

    out[0] = (
        dot(stacked[0], weights[1], ((1,), (1,)))
        + dot(stacked[1], weights[2], ((1,), (1,)))
        + dot(gate_grad[...], weights[3], ((1,), (1,)))
    )


def project_late_kernel(place, query_own, query_other, early, weights, out, stacked):
    @pl.when(pl.program_id(0) == 0)
    def _():
        own = pl.ds(pl.multiple_of(place[0] * HEAD_DIM, HEAD_DIM), HEAD_DIM)
        other = pl.ds(pl.multiple_of((1 - place[0]) * HEAD_DIM, HEAD_DIM), HEAD_DIM)
        stacked[:, own] = query_own[...]
        stacked[:, other] = query_other[...]

    out[0] = (early[0] + dot(stacked[...], weights[0], ((1,), (1,)))).astype(out.dtype)


def project(place, skip, count, grads, early, projections, dtype):
    width = projections.shape[2]
    rows = grads[0].shape[-2]
    whole = lambda array: pl.BlockSpec(array.shape, lambda i, place: (0,) * array.ndim)
    if early is None:
        kernel, deep, stacked = project_early_kernel, 4, (2, rows, width)
        partial = []
    else:
        kernel, deep, stacked = project_late_kernel, 1, (rows, width)
        partial = [pl.BlockSpec((1, rows, width), lambda i, place: (skip + i, 0, 0))]
    return pl.pallas_call(
        kernel,
        grid_spec=pltpu.PrefetchScalarGridSpec(
            num_scalar_prefetch=1,
            grid=(count,),
            in_specs=[whole(grad) for grad in grads]
            + partial
            + [pl.BlockSpec((deep, width, width), lambda i, place: (0, place[1 + skip + i], 0))],
            out_specs=pl.BlockSpec((1, rows, width), lambda i, place: (i, 0, 0)),
            scratch_shapes=[pltpu.VMEM(stacked, BF16)],
        ),
        out_shape=jax.ShapeDtypeStruct((count, rows, width), dtype),
        compiler_params=pltpu.CompilerParams(vmem_limit_bytes=VMEM_BYTES),
        cost_estimate=pl.CostEstimate(
            flops=2 * deep * count * rows * width * width,
            bytes_accessed=rows * width * (8 + 4 * count),
            transcendentals=0,
        ),
        name="project_early" if early is None else "project_late",
    )(place, *grads, *([] if early is None else [early]), projections)


def per_device(queries, key_rows, value_rows, attn_out, gate_pre, out_grad, segments, projections):
    rows = queries.shape[0]
    shards, groups = lax.axis_size("seq"), lax.axis_size("head")
    shard, group = lax.axis_index("seq"), lax.axis_index("head")
    pairs = shards // PAIR
    pair, lane = shard // PAIR, shard % PAIR

    def shift(block, distance, cross=0):
        route = [(i, (i + PAIR * distance) ^ cross) for i in range(shards)]
        return lax.ppermute(block, "seq", [hop for hop in route if 0 <= hop[1] < shards])

    query_own, query_other, key_own, key_other, gate_grad, seg_all = prepare(
        shards, queries, key_rows, value_rows, attn_out, gate_pre, out_grad,
        segments.reshape(-1, HEAD_DIM),
    )
    segs = seg_all.reshape(shards * rows)
    seg_rows = seg_all.reshape(shards, rows).astype(F32)
    block_a, block_b = query_own, shift(query_other, 0, 1)
    keys = (key_own, shift(key_other, 0, 1))

    reach = min((WINDOW + 1) // PAIR, pairs - 1)
    acc, own_sum, other_sum = None, None, None
    for distance in range(reach + 1):
        if distance > 0:
            block_a, block_b = shift(block_a, -1), shift(block_b, -1)
        far = PAIR * jnp.minimum(pair + distance, pairs - 1)
        ids = jnp.stack(
            [far + lane, far + 1 - lane, shard, shard ^ 1, (pair + distance < pairs)]
        ).astype(jnp.int32)
        part_own, part_other, acc_own, acc_other = attend(
            distance == 0, distance == reach, ids, segs, seg_rows, (block_a, block_b), keys, acc
        )
        acc = (acc_own, acc_other)
        part_other = shift(part_other, distance, 1).astype(F32)
        if distance == 0:
            own_sum, other_sum = part_own, part_other
        else:
            own_sum = own_sum + shift(part_own, distance).astype(F32)
            other_sum = other_sum + part_other
    late = (own_sum.astype(BF16), other_sum.astype(BF16))
    early = (acc[0], shift(acc[1], 0, 1), gate_grad)

    bits = []
    while (1 << len(bits)) < groups:
        bits.append(1 << len(bits))
    kept = list(range(groups))

    def across(block, bit):
        return lax.ppermute(block, "head", [(i, i ^ bit) for i in range(groups)])

    sent = [offset for offset in kept if offset & 1 == 1]
    near = [offset for offset in kept if offset & 1 == 0]
    place = jnp.stack([lane] + [group ^ offset for offset in sent + near]).astype(jnp.int32)
    base = project(place, 0, groups, early, None, projections, F32)
    away = project(place, 0, len(sent), late, base, projections, BF16)
    arrived = across(away, 1)
    total = project(place, len(sent), len(near), late, base, projections, F32)
    total = total + arrived.astype(F32)
    for bit in bits[1:]:
        sent = [n for n, offset in enumerate(near) if offset & bit]
        held = [n for n, offset in enumerate(near) if not offset & bit]
        arrived = across(jnp.stack([total[n] for n in sent]).astype(BF16), bit)
        total = jnp.stack([total[n] for n in held]) + arrived.astype(F32)
        near = [near[n] for n in held]
    return total[0].astype(BF16)


def solution(mesh):
    return jax.shard_map(
        per_device,
        mesh=mesh,
        in_specs=(
            P("seq", "head"),
            P("seq", "head"),
            P("seq", "head"),
            P("seq", "head"),
            P("seq", "head"),
            P("seq", "head"),
            P("seq"),
            P(None, None, "head"),
        ),
        out_specs=P("seq", "head"),
        check_vma=False,
    )
```

```python
import functools

import jax
import jax.numpy as jnp
from jax import lax
from jax.experimental import pallas as pl
from jax.experimental.pallas import tpu as pltpu
from jax.sharding import PartitionSpec as P

HEAD_DIM = 128
WINDOW = 6
PAIR = 2
TILE = 512
SCALE = HEAD_DIM ** (-0.5)
VMEM_BYTES = 60 * 2**20
BF16 = jnp.bfloat16
F32 = jnp.float32


def dot(left, right, dims):
    return lax.dot_general(left, right, (dims, ((), ())), preferred_element_type=F32)


def prepare_kernel(
    shards, queries, keys, values, attn_out, gate_pre, out_grad, segments,
    query_own, key_own, other, gate_grad, seg_all, send_sems, recv_sems,
):
    me = lax.axis_index("seq")
    lane = lax.rem(me, PAIR)
    step = pl.program_id(0)

    def seg_copies():
        return [
            pltpu.make_async_remote_copy(
                src_ref=segments,
                dst_ref=seg_all.at[me],
                send_sem=send_sems.at[offset],
                recv_sem=recv_sems.at[offset],
                device_id={"seq": lax.rem(me + offset, shards)},
                device_id_type=pl.DeviceIdType.MESH,
            )
            for offset in range(1, shards)
        ]

    @pl.when(step == 0)
    def _():
        barrier = pltpu.get_barrier_semaphore()
        for offset in range(1, shards):
            pl.semaphore_signal(
                barrier,
                inc=1,
                device_id={"seq": lax.rem(me + offset, shards)},
                device_id_type=pl.DeviceIdType.MESH,
            )

    @pl.when(step == 1)
    def _():
        pl.semaphore_wait(pltpu.get_barrier_semaphore(), shards - 1)
        for copy in seg_copies():
            copy.start()
        own = pltpu.make_async_copy(segments, seg_all.at[me], send_sems.at[0])
        own.start()
        own.wait()

    for slot, (to_query, to_key) in enumerate(
        ((query_own, key_own), (other.at[pl.ds(0, 2)], other.at[pl.ds(2, 2)]))
    ):
        head = lane if slot == 0 else 1 - lane
        cols = pl.ds(pl.multiple_of(head * HEAD_DIM, HEAD_DIM), HEAD_DIM)
        to_query[0] = queries[:, cols]
        to_key[0] = keys[:, cols]
        to_key[1] = values[:, cols]
        saved = attn_out[:, cols].astype(F32)
        centred = saved - jnp.mean(saved, axis=-1, keepdims=True)
        inverse = lax.rsqrt(jnp.mean(centred * centred, axis=-1, keepdims=True) + 1e-06)
        normed = centred * inverse
        gate_in = gate_pre[:, cols].astype(F32)
        grad_in = out_grad[:, cols].astype(F32)
        sigma = jax.nn.sigmoid(gate_in)
        gate_grad[:, cols] = (
            grad_in * normed * (sigma * (1.0 + gate_in * (1.0 - sigma)))
        ).astype(BF16)
        normed_grad = grad_in * (gate_in * sigma)
        to_query[1] = (
            inverse
            * (
                normed_grad
                - jnp.mean(normed_grad, axis=-1, keepdims=True)
                - normed * jnp.mean(normed_grad * normed, axis=-1, keepdims=True)
            )
        ).astype(BF16)

    @pl.when(step == pl.num_programs(0) - 1)
    def _():
        for copy in seg_copies():
            copy.wait()


def prepare(shards, queries, keys, values, attn_out, gate_pre, out_grad, segments):
    rows, width = queries.shape
    step = min(rows // 2, 256)
    wide = pl.BlockSpec((step, width), lambda i: (i, 0))
    heads = lambda deep: pl.BlockSpec((deep, step, HEAD_DIM), lambda i: (0, i, 0))
    head_shape = lambda deep: jax.ShapeDtypeStruct((deep, rows, HEAD_DIM), BF16)
    any_spec = pl.BlockSpec(memory_space=pl.ANY)
    return pl.pallas_call(
        functools.partial(prepare_kernel, shards),
        grid=(rows // step,),
        in_specs=[wide] * 6 + [any_spec],
        out_specs=[heads(2), heads(2), heads(4), wide, any_spec],
        out_shape=[
            head_shape(2),
            head_shape(2),
            head_shape(4),
            jax.ShapeDtypeStruct((rows, width), BF16),
            jax.ShapeDtypeStruct((shards,) + segments.shape, segments.dtype),
        ],
        scratch_shapes=[
            pltpu.SemaphoreType.DMA((shards,)),
            pltpu.SemaphoreType.DMA((shards,)),
        ],
        compiler_params=pltpu.CompilerParams(
            vmem_limit_bytes=VMEM_BYTES, collective_id=0, has_side_effects=True
        ),
        cost_estimate=pl.CostEstimate(
            flops=40 * rows * width, bytes_accessed=22 * rows * width, transcendentals=rows * width
        ),
        name="prepare",
    )(queries, keys, values, attn_out, gate_pre, out_grad, segments)


def attend_kernel(plan, first, last, ids, segs, seg_rows, *refs):
    blocks, refs = refs[: len(plan.blocks)], refs[len(plan.blocks) :]
    if not first:
        accs, refs = refs[:2], refs[2:]
    outs, (held, query_acc, key_acc, sems) = refs[:2], refs[2:]
    rows = held.shape[2]
    per = rows // TILE

    copies = [
        pltpu.make_async_copy(block, held.at[n], sems.at[n]) for n, block in enumerate(blocks)
    ]
    if first:
        query_acc[...] = jnp.zeros_like(query_acc)
        key_acc[...] = jnp.zeros_like(key_acc)
    else:
        copies += [
            pltpu.make_async_copy(source, target, sems.at[len(blocks) + n])
            for n, (source, target) in enumerate(zip(accs, (query_acc, key_acc)))
        ]
    for copy in copies:
        copy.start()
    for copy in copies:
        copy.wait()

    def run(q_start, q_count, k_start, k_count, to_query, to_key):
        k_tiles = k_count * per

        def body(index, carry):
            q_idx, k_idx = index // k_tiles, index % k_tiles
            q_blk, k_blk = q_idx // per, k_idx // per
            q_off = pl.multiple_of((q_idx % per) * TILE, TILE)
            k_off = pl.multiple_of((k_idx % per) * TILE, TILE)
            q_held, k_held = q_start + q_blk, k_start + k_blk
            valid = (ids[q_held] >= 0) & (ids[k_held] >= 0)
            q_shard, k_shard = jnp.maximum(ids[q_held], 0), jnp.maximum(ids[k_held], 0)
            q_first, k_first = q_shard * rows + q_off, k_shard * rows + k_off
            q_last, k_last = q_first + TILE - 1, k_first + TILE - 1
            live = valid & (k_first <= q_last) & (segs[k_last] >= segs[q_first])
            full = (k_last <= q_first) & (segs[k_first] == segs[q_last])
            q_rows, k_rows = pl.ds(q_off, TILE), pl.ds(k_off, TILE)

            def work(masked):
                query = held[q_held, 0, q_rows, :]
                grad = held[q_held, 1, q_rows, :]
                key = held[k_held, 0, k_rows, :]
                value = held[k_held, 1, k_rows, :]
                half = dot(key, query, ((1,), (1,))) * (SCALE / 2)
                slope_in = dot(value, grad, ((1,), (1,)))
                tanh = jnp.tanh(half)
                upper = 1.0 + tanh
                weights = half * upper
                score_grad = slope_in * (upper + weights * (1.0 - tanh))
                if masked:
                    seg_q = seg_rows[pl.ds(q_shard, 1), q_rows]
                    seg_k = seg_rows[pl.ds(k_shard, 1), k_rows]
                    seg_k = jnp.transpose(jnp.broadcast_to(seg_k, (HEAD_DIM, TILE)))[:, :1]
                    place_k = k_first + lax.broadcasted_iota(jnp.int32, (TILE, TILE), 0)
                    place_q = q_first + lax.broadcasted_iota(jnp.int32, (TILE, TILE), 1)
                    allowed = (seg_q == seg_k) & (place_k <= place_q)
                    weights = jnp.where(allowed, weights, 0.0)
                    score_grad = jnp.where(allowed, score_grad, 0.0)
                score_grad = score_grad.astype(BF16)
                if to_key:
                    weights = weights.astype(BF16)
                    key_acc[k_blk, 0, k_rows, :] += dot(score_grad, query, ((1,), (0,)))
                    key_acc[k_blk, 1, k_rows, :] += dot(weights, grad, ((1,), (0,)))
                if to_query:
                    query_acc[q_blk, q_rows, :] += dot(score_grad, key, ((0,), (0,)))

            @pl.when(live & full)
            def _():
                work(False)

            @pl.when(live & jnp.logical_not(full))
            def _():
                work(True)

            return carry

        lax.fori_loop(0, q_count * per * k_tiles, body, 0)

    for entry in plan.entries:
        run(*entry)
    if last:
        for blk, out in enumerate(outs):
            out[0] = (query_acc[blk] * (SCALE / 2)).astype(BF16)
            out[1] = (key_acc[blk, 0] * (SCALE / 2)).astype(BF16)
            out[2] = key_acc[blk, 1].astype(BF16)
    else:
        done = [
            pltpu.make_async_copy(source, target, sems.at[n])
            for n, (source, target) in enumerate(zip((query_acc, key_acc), outs))
        ]
        for copy in done:
            copy.start()
        for copy in done:
            copy.wait()


class Plan:
    def __init__(self, shards):
        self.blocks, self.ids, self.entries = [], [], []
        self.shards = shards

    def add(self, blocks, ids):
        start = len(self.blocks)
        self.blocks += blocks
        self.ids += ids
        return start, len(blocks)


def attend(plan, first, last, segs, seg_rows, acc):
    rows = plan.blocks[0].shape[1]
    any_spec = pl.BlockSpec(memory_space=pl.ANY)
    vmem = pl.BlockSpec(memory_space=pltpu.VMEM)
    ids = jnp.stack(plan.ids).astype(jnp.int32)
    acc = [] if first else list(acc)
    query_shape, key_shape = (2, rows, HEAD_DIM), (2, 2, rows, HEAD_DIM)
    if last:
        out_shape = [jax.ShapeDtypeStruct((3, rows, HEAD_DIM), BF16)] * 2
    else:
        out_shape = [jax.ShapeDtypeStruct(query_shape, F32), jax.ShapeDtypeStruct(key_shape, F32)]
    return pl.pallas_call(
        functools.partial(attend_kernel, plan, first, last),
        grid_spec=pltpu.PrefetchScalarGridSpec(
            num_scalar_prefetch=2,
            grid=(),
            in_specs=[vmem] + [any_spec] * (len(plan.blocks) + len(acc)),
            out_specs=[vmem if last else any_spec] * 2,
            scratch_shapes=[
                pltpu.VMEM((len(plan.blocks), 2, rows, HEAD_DIM), BF16),
                pltpu.VMEM(query_shape, F32),
                pltpu.VMEM(key_shape, F32),
                pltpu.SemaphoreType.DMA((len(plan.blocks) + 2,)),
            ],
        ),
        out_shape=out_shape,
        compiler_params=pltpu.CompilerParams(vmem_limit_bytes=VMEM_BYTES),
        cost_estimate=pl.CostEstimate(
            flops=2 * rows * rows * HEAD_DIM, bytes_accessed=8 * rows * HEAD_DIM, transcendentals=0
        ),
        name="attend",
    )(ids, segs, seg_rows, *plan.blocks, *acc)


def project_early_kernel(place, own, gate_grad, weights, out):
    cols = pl.ds(pl.multiple_of(place[0] * HEAD_DIM, HEAD_DIM), HEAD_DIM)
    total = dot(gate_grad[...], weights[3], ((1,), (1,)))
    for part in range(3):
        total = total + dot(own[part], weights[part, :, cols], ((1,), (1,)))
    out[0] = total


def project_late_kernel(place, other, early, weights, out):
    cols = pl.ds(pl.multiple_of((1 - place[0]) * HEAD_DIM, HEAD_DIM), HEAD_DIM)
    total = early[0]
    for part in range(3):
        total = total + dot(other[part], weights[part, :, cols], ((1,), (1,)))
    out[0] = total.astype(out.dtype)


def project(place, skip, count, grads, early, projections, dtype):
    width = projections.shape[2]
    rows = grads[0].shape[-2]
    whole = lambda array: pl.BlockSpec(array.shape, lambda i, place: (0,) * array.ndim)
    partial = []
    if early is not None:
        partial = [pl.BlockSpec((1, rows, width), lambda i, place: (skip + i, 0, 0))]
    return pl.pallas_call(
        project_early_kernel if early is None else project_late_kernel,
        grid_spec=pltpu.PrefetchScalarGridSpec(
            num_scalar_prefetch=1,
            grid=(count,),
            in_specs=[whole(grad) for grad in grads]
            + partial
            + [pl.BlockSpec((4, width, width), lambda i, place: (0, place[1 + skip + i], 0))],
            out_specs=pl.BlockSpec((1, rows, width), lambda i, place: (i, 0, 0)),
        ),
        out_shape=jax.ShapeDtypeStruct((count, rows, width), dtype),
        compiler_params=pltpu.CompilerParams(vmem_limit_bytes=VMEM_BYTES),
        cost_estimate=pl.CostEstimate(
            flops=6 * count * rows * width * width,
            bytes_accessed=rows * width * (8 + 4 * count),
            transcendentals=0,
        ),
        name="project_early" if early is None else "project_late",
    )(place, *grads, *([] if early is None else [early]), projections)


def per_device(queries, key_rows, value_rows, attn_out, gate_pre, out_grad, segments, projections):
    rows = queries.shape[0]
    shards, groups = lax.axis_size("seq"), lax.axis_size("head")
    shard, group = lax.axis_index("seq"), lax.axis_index("head")
    pairs = shards // PAIR
    pair, lane = shard // PAIR, shard % PAIR

    def shift(block, distance, cross=0):
        route = [(i, (i + PAIR * distance) ^ cross) for i in range(shards)]
        return lax.ppermute(block, "seq", [hop for hop in route if 0 <= hop[1] < shards])

    query_own, key_own, other, gate_grad, seg_all = prepare(
        shards, queries, key_rows, value_rows, attn_out, gate_pre, out_grad,
        segments.reshape(-1, HEAD_DIM),
    )
    segs = seg_all.reshape(shards * rows)
    seg_rows = seg_all.reshape(shards, rows).astype(F32)
    reach = min((WINDOW + 1) // PAIR, pairs - 1)

    def travel(block, sign, relay):
        arrived = {0: block}
        for distance in range(1, reach + 1):
            if relay:
                arrived[distance] = shift(arrived[distance - 1], sign)
            else:
                arrived[distance] = shift(block, sign * distance)
        return arrived

    partner = shift(other, 0, 1)
    query_mine = [query_own, partner[:2]]
    key_mine = [key_own, partner[2:]]
    here = [shard, shard ^ 1]
    far_queries = [travel(block, -1, relay) for block, relay in zip(query_mine, (True, False))]
    far_keys = [travel(block, 1, relay) for block, relay in zip(key_mine, (True, False))]

    def far_ids(distance):
        far = pair + distance
        valid = (far >= 0) & (far < pairs)
        return [jnp.where(valid, PAIR * far + spot, -1) for spot in (lane, 1 - lane)]

    acc = None
    stages = [[0]] + [[distance] for distance in range(1, min(reach, 1) + 1)]
    if reach > 1:
        stages.append(list(range(2, reach + 1)))
    for number, stage in enumerate(stages):
        plan = Plan(shards)
        query_at = plan.add(query_mine, here)
        key_at = plan.add(key_mine, here)
        if number == 0:
            plan.entries.append((*query_at, *key_at, True, True))
        else:
            queries_in, keys_in, query_ids, key_ids = [], [], [], []
            for distance in stage:
                queries_in += [blocks[distance] for blocks in far_queries]
                keys_in += [blocks[distance] for blocks in far_keys]
                query_ids += far_ids(distance)
                key_ids += far_ids(-distance)
            plan.entries.append((*plan.add(queries_in, query_ids), *key_at, False, True))
            plan.entries.append((*query_at, *plan.add(keys_in, key_ids), True, False))
        acc = attend(plan, number == 0, number == len(stages) - 1, segs, seg_rows, acc)
    own_grads, other_grads = acc
    early = (own_grads, gate_grad)
    late = (shift(other_grads, 0, 1),)

    bits = []
    while (1 << len(bits)) < groups:
        bits.append(1 << len(bits))
    kept = list(range(groups))

    def across(block, bit):
        return lax.ppermute(block, "head", [(i, i ^ bit) for i in range(groups)])

    sent = [offset for offset in kept if offset & 1 == 1]
    near = [offset for offset in kept if offset & 1 == 0]
    place = jnp.stack([lane] + [group ^ offset for offset in sent + near]).astype(jnp.int32)
    base = project(place, 0, groups, early, None, projections, F32)
    away = project(place, 0, len(sent), late, base, projections, BF16)
    arrived = across(away, 1)
    total = project(place, len(sent), len(near), late, base, projections, F32)
    total = total + arrived.astype(F32)
    for bit in bits[1:]:
        sent = [n for n, offset in enumerate(near) if offset & bit]
        held = [n for n, offset in enumerate(near) if not offset & bit]
        arrived = across(jnp.stack([total[n] for n in sent]).astype(BF16), bit)
        total = jnp.stack([total[n] for n in held]) + arrived.astype(F32)
        near = [near[n] for n in held]
    return total[0].astype(BF16)


def solution(mesh):
    return jax.shard_map(
        per_device,
        mesh=mesh,
        in_specs=(
            P("seq", "head"),
            P("seq", "head"),
            P("seq", "head"),
            P("seq", "head"),
            P("seq", "head"),
            P("seq", "head"),
            P("seq"),
            P(None, None, "head"),
        ),
        out_specs=P("seq", "head"),
        check_vma=False,
    )
```

```python
import functools

import jax
import jax.numpy as jnp
from jax import lax
from jax.experimental import pallas as pl
from jax.experimental.pallas import tpu as pltpu
from jax.sharding import PartitionSpec as P

HEAD_DIM = 128
WINDOW = 6
PAIR = 2
TILE = 512
SCALE = HEAD_DIM ** (-0.5)
VMEM_BYTES = 60 * 2**20
BF16 = jnp.bfloat16
F32 = jnp.float32


def dot(left, right, dims):
    return lax.dot_general(left, right, (dims, ((), ())), preferred_element_type=F32)


def share_kernel(shards, segments, after, seg_all, send_sems, recv_sems):
    me = lax.axis_index("seq")
    to = [{"seq": lax.rem(me + offset, shards)} for offset in range(shards)]
    barrier = pltpu.get_barrier_semaphore()
    for offset in range(1, shards):
        pl.semaphore_signal(
            barrier, inc=1, device_id=to[offset], device_id_type=pl.DeviceIdType.MESH
        )
    pl.semaphore_wait(barrier, shards - 1)
    copies = [
        pltpu.make_async_remote_copy(
            src_ref=segments,
            dst_ref=seg_all.at[me],
            send_sem=send_sems.at[offset],
            recv_sem=recv_sems.at[offset],
            device_id=to[offset],
            device_id_type=pl.DeviceIdType.MESH,
        )
        for offset in range(1, shards)
    ]
    copies.append(pltpu.make_async_copy(segments, seg_all.at[me], send_sems.at[0]))
    for copy in copies:
        copy.start()
    for copy in copies:
        copy.wait()


def share(shards, segments, after):
    any_spec = pl.BlockSpec(memory_space=pl.ANY)
    return pl.pallas_call(
        functools.partial(share_kernel, shards),
        in_specs=[any_spec] * 2,
        out_specs=any_spec,
        out_shape=jax.ShapeDtypeStruct((shards,) + segments.shape, segments.dtype),
        scratch_shapes=[
            pltpu.SemaphoreType.DMA((shards,)),
            pltpu.SemaphoreType.DMA((shards,)),
        ],
        compiler_params=pltpu.CompilerParams(
            vmem_limit_bytes=VMEM_BYTES, collective_id=0, has_side_effects=True
        ),
        cost_estimate=pl.CostEstimate(
            flops=0, bytes_accessed=2 * shards * segments.size * 4, transcendentals=0
        ),
        name="share",
    )(segments, after)


def prepare_kernel(
    queries, keys, values, attn_out, gate_pre, out_grad, query_own, key_own, other, gate_grad
):
    lane = lax.rem(lax.axis_index("seq"), PAIR)
    for slot, (to_query, to_key) in enumerate(
        ((query_own, key_own), (other.at[pl.ds(0, 2)], other.at[pl.ds(2, 2)]))
    ):
        head = lane if slot == 0 else 1 - lane
        cols = pl.ds(pl.multiple_of(head * HEAD_DIM, HEAD_DIM), HEAD_DIM)
        to_query[0] = queries[:, cols]
        to_key[0] = keys[:, cols]
        to_key[1] = values[:, cols]
        saved = attn_out[:, cols].astype(F32)
        centred = saved - jnp.mean(saved, axis=-1, keepdims=True)
        inverse = lax.rsqrt(jnp.mean(centred * centred, axis=-1, keepdims=True) + 1e-06)
        normed = centred * inverse
        gate_in = gate_pre[:, cols].astype(F32)
        grad_in = out_grad[:, cols].astype(F32)
        sigma = jax.nn.sigmoid(gate_in)
        gate_grad[:, cols] = (
            grad_in * normed * (sigma * (1.0 + gate_in * (1.0 - sigma)))
        ).astype(BF16)
        normed_grad = grad_in * (gate_in * sigma)
        to_query[1] = (
            inverse
            * (
                normed_grad
                - jnp.mean(normed_grad, axis=-1, keepdims=True)
                - normed * jnp.mean(normed_grad * normed, axis=-1, keepdims=True)
            )
        ).astype(BF16)


def prepare(queries, keys, values, attn_out, gate_pre, out_grad):
    rows, width = queries.shape
    step = min(rows // 2, 256)
    wide = pl.BlockSpec((step, width), lambda i: (i, 0))
    heads = lambda deep: pl.BlockSpec((deep, step, HEAD_DIM), lambda i: (0, i, 0))
    head_shape = lambda deep: jax.ShapeDtypeStruct((deep, rows, HEAD_DIM), BF16)
    return pl.pallas_call(
        prepare_kernel,
        grid=(rows // step,),
        in_specs=[wide] * 6,
        out_specs=[heads(2), heads(2), heads(4), wide],
        out_shape=[
            head_shape(2),
            head_shape(2),
            head_shape(4),
            jax.ShapeDtypeStruct((rows, width), BF16),
        ],
        compiler_params=pltpu.CompilerParams(vmem_limit_bytes=VMEM_BYTES),
        cost_estimate=pl.CostEstimate(
            flops=40 * rows * width, bytes_accessed=22 * rows * width, transcendentals=rows * width
        ),
        name="prepare",
    )(queries, keys, values, attn_out, gate_pre, out_grad)


def attend_kernel(plan, first, last, ids, segs, seg_rows, *refs):
    blocks, refs = refs[: len(plan.blocks)], refs[len(plan.blocks) :]
    if not first:
        accs, refs = refs[:2], refs[2:]
    outs, (held, query_acc, key_acc, sems) = refs[:2], refs[2:]
    rows = held.shape[2]
    per = rows // TILE

    copies = [
        pltpu.make_async_copy(block, held.at[n], sems.at[n]) for n, block in enumerate(blocks)
    ]
    if first:
        query_acc[...] = jnp.zeros_like(query_acc)
        key_acc[...] = jnp.zeros_like(key_acc)
    else:
        copies += [
            pltpu.make_async_copy(source, target, sems.at[len(blocks) + n])
            for n, (source, target) in enumerate(zip(accs, (query_acc, key_acc)))
        ]
    for copy in copies:
        copy.start()
    waiting = set(range(len(copies)))

    def arrive(needed):
        for n in sorted(waiting & set(needed)):
            copies[n].wait()
            waiting.discard(n)

    arrive(range(len(blocks), len(copies)))

    def run(q_start, q_count, k_start, k_count, to_query, to_key):
        arrive(range(q_start, q_start + q_count))
        arrive(range(k_start, k_start + k_count))

        def pair_body(index, carry):
            q_blk, k_blk = index // k_count, index % k_count
            q_shard, k_shard = ids[q_start + q_blk], ids[k_start + k_blk]
            valid = (q_shard >= 0) & (k_shard >= 0) & (k_shard <= q_shard)
            q_shard, k_shard = jnp.maximum(q_shard, 0), jnp.maximum(k_shard, 0)
            meet = segs[k_shard * rows + rows - 1] >= segs[q_shard * rows]

            @pl.when(valid & meet)
            def _():
                lax.fori_loop(
                    0, per * per, functools.partial(tile_body, q_blk, k_blk, q_shard, k_shard), 0
                )

            return carry

        def tile_body(q_blk, k_blk, q_shard, k_shard, index, carry):
            q_off = pl.multiple_of((index // per) * TILE, TILE)
            k_off = pl.multiple_of((index % per) * TILE, TILE)
            q_held, k_held = q_start + q_blk, k_start + k_blk
            q_first, k_first = q_shard * rows + q_off, k_shard * rows + k_off
            q_last, k_last = q_first + TILE - 1, k_first + TILE - 1
            live = (k_first <= q_last) & (segs[k_last] >= segs[q_first])
            full = (k_last <= q_first) & (segs[k_first] == segs[q_last])
            q_rows, k_rows = pl.ds(q_off, TILE), pl.ds(k_off, TILE)

            def work(masked):
                query = held[q_held, 0, q_rows, :]
                grad = held[q_held, 1, q_rows, :]
                key = held[k_held, 0, k_rows, :]
                value = held[k_held, 1, k_rows, :]
                half = dot(key, query, ((1,), (1,))) * (SCALE / 2)
                slope_in = dot(value, grad, ((1,), (1,)))
                tanh = jnp.tanh(half)
                upper = 1.0 + tanh
                weights = half * upper
                score_grad = slope_in * (upper + weights * (1.0 - tanh))
                if masked:
                    seg_q = seg_rows[pl.ds(q_shard, 1), q_rows]
                    seg_k = seg_rows[pl.ds(k_shard, 1), k_rows]
                    seg_k = jnp.transpose(jnp.broadcast_to(seg_k, (HEAD_DIM, TILE)))[:, :1]
                    place_k = k_first + lax.broadcasted_iota(jnp.int32, (TILE, TILE), 0)
                    place_q = q_first + lax.broadcasted_iota(jnp.int32, (TILE, TILE), 1)
                    allowed = (seg_q == seg_k) & (place_k <= place_q)
                    weights = jnp.where(allowed, weights, 0.0)
                    score_grad = jnp.where(allowed, score_grad, 0.0)
                score_grad = score_grad.astype(BF16)
                if to_key:
                    weights = weights.astype(BF16)
                    key_acc[k_blk, 0, k_rows, :] += dot(score_grad, query, ((1,), (0,)))
                    key_acc[k_blk, 1, k_rows, :] += dot(weights, grad, ((1,), (0,)))
                if to_query:
                    query_acc[q_blk, q_rows, :] += dot(score_grad, key, ((0,), (0,)))

            @pl.when(live & full)
            def _():
                work(False)

            @pl.when(live & jnp.logical_not(full))
            def _():
                work(True)

            return carry

        lax.fori_loop(0, q_count * k_count, pair_body, 0)

    for entry in plan.entries:
        run(*entry)
    if last:
        for blk, out in enumerate(outs):
            out[0] = (query_acc[blk] * (SCALE / 2)).astype(BF16)
            out[1] = (key_acc[blk, 0] * (SCALE / 2)).astype(BF16)
            out[2] = key_acc[blk, 1].astype(BF16)
    else:
        done = [
            pltpu.make_async_copy(source, target, sems.at[n])
            for n, (source, target) in enumerate(zip((query_acc, key_acc), outs))
        ]
        for copy in done:
            copy.start()
        for copy in done:
            copy.wait()


class Plan:
    def __init__(self, shards):
        self.blocks, self.ids, self.entries = [], [], []
        self.shards = shards

    def add(self, blocks, ids):
        start = len(self.blocks)
        self.blocks += blocks
        self.ids += ids
        return start, len(blocks)


def attend(plan, first, last, segs, seg_rows, acc):
    rows = plan.blocks[0].shape[1]
    any_spec = pl.BlockSpec(memory_space=pl.ANY)
    vmem = pl.BlockSpec(memory_space=pltpu.VMEM)
    ids = jnp.stack(plan.ids).astype(jnp.int32)
    acc = [] if first else list(acc)
    query_shape, key_shape = (2, rows, HEAD_DIM), (2, 2, rows, HEAD_DIM)
    if last:
        out_shape = [jax.ShapeDtypeStruct((3, rows, HEAD_DIM), BF16)] * 2
    else:
        out_shape = [jax.ShapeDtypeStruct(query_shape, F32), jax.ShapeDtypeStruct(key_shape, F32)]
    return pl.pallas_call(
        functools.partial(attend_kernel, plan, first, last),
        grid_spec=pltpu.PrefetchScalarGridSpec(
            num_scalar_prefetch=2,
            grid=(),
            in_specs=[vmem] + [any_spec] * (len(plan.blocks) + len(acc)),
            out_specs=[vmem if last else any_spec] * 2,
            scratch_shapes=[
                pltpu.VMEM((len(plan.blocks), 2, rows, HEAD_DIM), BF16),
                pltpu.VMEM(query_shape, F32),
                pltpu.VMEM(key_shape, F32),
                pltpu.SemaphoreType.DMA((len(plan.blocks) + 2,)),
            ],
        ),
        out_shape=out_shape,
        compiler_params=pltpu.CompilerParams(vmem_limit_bytes=VMEM_BYTES),
        cost_estimate=pl.CostEstimate(
            flops=(1 if first else 2) * 2**7 * rows * rows * HEAD_DIM,
            bytes_accessed=16 * rows * HEAD_DIM * len(plan.blocks),
            transcendentals=4 * rows * rows,
        ),
        name="attend",
    )(ids, segs, seg_rows, *plan.blocks, *acc)


def project_early_kernel(place, own, gate_grad, weights, out):
    cols = pl.ds(pl.multiple_of(place[0] * HEAD_DIM, HEAD_DIM), HEAD_DIM)
    total = dot(gate_grad[...], weights[3], ((1,), (1,)))
    for part in range(3):
        total = total + dot(own[part], weights[part, :, cols], ((1,), (1,)))
    out[0] = total


def project_late_kernel(place, other, early, weights, out):
    cols = pl.ds(pl.multiple_of((1 - place[0]) * HEAD_DIM, HEAD_DIM), HEAD_DIM)
    total = early[0]
    for part in range(3):
        total = total + dot(other[part], weights[part, :, cols], ((1,), (1,)))
    out[0] = total.astype(out.dtype)


def project(place, skip, count, grads, early, projections, dtype):
    width = projections.shape[2]
    rows = grads[0].shape[-2]
    whole = lambda array: pl.BlockSpec(array.shape, lambda i, place: (0,) * array.ndim)
    partial = []
    if early is not None:
        partial = [pl.BlockSpec((1, rows, width), lambda i, place: (skip + i, 0, 0))]
    return pl.pallas_call(
        project_early_kernel if early is None else project_late_kernel,
        grid_spec=pltpu.PrefetchScalarGridSpec(
            num_scalar_prefetch=1,
            grid=(count,),
            in_specs=[whole(grad) for grad in grads]
            + partial
            + [pl.BlockSpec((4, width, width), lambda i, place: (0, place[1 + skip + i], 0))],
            out_specs=pl.BlockSpec((1, rows, width), lambda i, place: (i, 0, 0)),
        ),
        out_shape=jax.ShapeDtypeStruct((count, rows, width), dtype),
        compiler_params=pltpu.CompilerParams(vmem_limit_bytes=VMEM_BYTES),
        cost_estimate=pl.CostEstimate(
            flops=6 * count * rows * width * width,
            bytes_accessed=rows * width * (8 + 4 * count),
            transcendentals=0,
        ),
        name="project_early" if early is None else "project_late",
    )(place, *grads, *([] if early is None else [early]), projections)


def per_device(queries, key_rows, value_rows, attn_out, gate_pre, out_grad, segments, projections):
    rows = queries.shape[0]
    shards, groups = lax.axis_size("seq"), lax.axis_size("head")
    shard, group = lax.axis_index("seq"), lax.axis_index("head")
    pairs = shards // PAIR
    pair, lane = shard // PAIR, shard % PAIR

    def shift(block, distance, cross=0):
        route = [(i, (i + PAIR * distance) ^ cross) for i in range(shards)]
        return lax.ppermute(block, "seq", [hop for hop in route if 0 <= hop[1] < shards])

    query_own, key_own, other, gate_grad = prepare(
        queries, key_rows, value_rows, attn_out, gate_pre, out_grad
    )
    seg_all = share(shards, segments.reshape(-1, HEAD_DIM), gate_grad)
    segs = seg_all.reshape(shards * rows)
    seg_rows = seg_all.reshape(shards, rows).astype(F32)
    reach = min((WINDOW + 1) // PAIR, pairs - 1)

    def travel(block, sign):
        arrived = {0: block}
        for distance in range(1, reach + 1):
            if distance == 2:
                arrived[distance] = shift(arrived[1], sign)
            else:
                arrived[distance] = shift(block, sign * distance)
        return arrived

    partner = shift(other, 0, 1)
    query_mine = [query_own, partner[:2]]
    key_mine = [key_own, partner[2:]]
    here = [shard, shard ^ 1]
    far_queries = [travel(block, -1) for block in query_mine]
    far_keys = [travel(block, 1) for block in key_mine]

    def far_ids(distance):
        far = pair + distance
        valid = (far >= 0) & (far < pairs)
        return [jnp.where(valid, PAIR * far + spot, -1) for spot in (lane, 1 - lane)]

    acc = None
    stages = [[0]] + [[distance] for distance in range(1, min(reach, 1) + 1)]
    if reach > 1:
        stages.append(list(range(2, reach + 1)))
    for number, stage in enumerate(stages):
        plan = Plan(shards)
        query_at = plan.add(query_mine, here)
        key_at = plan.add(key_mine, here)
        if number == 0:
            plan.entries.append((*query_at, *key_at, True, True))
        else:
            queries_in, keys_in, query_ids, key_ids = [], [], [], []
            for distance in stage:
                queries_in += [blocks[distance] for blocks in far_queries]
                keys_in += [blocks[distance] for blocks in far_keys]
                query_ids += far_ids(distance)
                key_ids += far_ids(-distance)
            plan.entries.append((*plan.add(queries_in, query_ids), *key_at, False, True))
            plan.entries.append((*query_at, *plan.add(keys_in, key_ids), True, False))
        acc = attend(plan, number == 0, number == len(stages) - 1, segs, seg_rows, acc)
    own_grads, other_grads = acc
    early = (own_grads, gate_grad)
    late = (shift(other_grads, 0, 1),)

    bits = []
    while (1 << len(bits)) < groups:
        bits.append(1 << len(bits))
    kept = list(range(groups))

    def across(block, bit):
        return lax.ppermute(block, "head", [(i, i ^ bit) for i in range(groups)])

    sent = [offset for offset in kept if offset & 1 == 1]
    near = [offset for offset in kept if offset & 1 == 0]
    place = jnp.stack([lane] + [group ^ offset for offset in sent + near]).astype(jnp.int32)
    base = project(place, 0, groups, early, None, projections, F32)
    away = project(place, 0, len(sent), late, base, projections, BF16)
    arrived = across(away, 1)
    total = project(place, len(sent), len(near), late, base, projections, F32)
    total = total + arrived.astype(F32)
    for bit in bits[1:]:
        sent = [n for n, offset in enumerate(near) if offset & bit]
        held = [n for n, offset in enumerate(near) if not offset & bit]
        arrived = across(jnp.stack([total[n] for n in sent]).astype(BF16), bit)
        total = jnp.stack([total[n] for n in held]) + arrived.astype(F32)
        near = [near[n] for n in held]
    return total[0].astype(BF16)


def solution(mesh):
    return jax.shard_map(
        per_device,
        mesh=mesh,
        in_specs=(
            P("seq", "head"),
            P("seq", "head"),
            P("seq", "head"),
            P("seq", "head"),
            P("seq", "head"),
            P("seq", "head"),
            P("seq"),
            P(None, None, "head"),
        ),
        out_specs=P("seq", "head"),
        check_vma=False,
    )
```

```python
import functools

import jax
import jax.numpy as jnp
from jax import lax
from jax.experimental import pallas as pl
from jax.experimental.pallas import tpu as pltpu
from jax.sharding import PartitionSpec as P

HEAD_DIM = 128
WINDOW = 6
PAIR = 2
TILE = 512
SCALE = HEAD_DIM ** (-0.5)
VMEM_BYTES = 60 * 2**20
BF16 = jnp.bfloat16
F32 = jnp.float32


def dot(left, right, dims):
    return lax.dot_general(left, right, (dims, ((), ())), preferred_element_type=F32)


def share_kernel(shards, segments, seg_all, send_sems, recv_sems):
    me = lax.axis_index("seq")
    to = [{"seq": lax.rem(me + offset, shards)} for offset in range(shards)]
    barrier = pltpu.get_barrier_semaphore()
    for offset in range(1, shards):
        pl.semaphore_signal(
            barrier, inc=1, device_id=to[offset], device_id_type=pl.DeviceIdType.MESH
        )
    pl.semaphore_wait(barrier, shards - 1)
    copies = [
        pltpu.make_async_remote_copy(
            src_ref=segments,
            dst_ref=seg_all.at[me],
            send_sem=send_sems.at[offset],
            recv_sem=recv_sems.at[offset],
            device_id=to[offset],
            device_id_type=pl.DeviceIdType.MESH,
        )
        for offset in range(1, shards)
    ]
    copies.append(pltpu.make_async_copy(segments, seg_all.at[me], send_sems.at[0]))
    for copy in copies:
        copy.start()
    for copy in copies:
        copy.wait()


def share(shards, segments):
    any_spec = pl.BlockSpec(memory_space=pl.ANY)
    return pl.pallas_call(
        functools.partial(share_kernel, shards),
        in_specs=[any_spec],
        out_specs=any_spec,
        out_shape=jax.ShapeDtypeStruct((shards,) + segments.shape, segments.dtype),
        scratch_shapes=[
            pltpu.SemaphoreType.DMA((shards,)),
            pltpu.SemaphoreType.DMA((shards,)),
        ],
        compiler_params=pltpu.CompilerParams(
            vmem_limit_bytes=VMEM_BYTES, collective_id=0, has_side_effects=True
        ),
        cost_estimate=pl.CostEstimate(
            flops=0, bytes_accessed=2 * shards * segments.size * 4, transcendentals=0
        ),
        name="share",
    )(segments)


def prepare_kernel(
    queries, keys, values, attn_out, gate_pre, out_grad, after,
    query_own, key_own, other, gate_grad,
):
    lane = lax.rem(lax.axis_index("seq"), PAIR)
    for slot, (to_query, to_key) in enumerate(
        ((query_own, key_own), (other.at[pl.ds(0, 2)], other.at[pl.ds(2, 2)]))
    ):
        head = lane if slot == 0 else 1 - lane
        cols = pl.ds(pl.multiple_of(head * HEAD_DIM, HEAD_DIM), HEAD_DIM)
        to_query[0] = queries[:, cols]
        to_key[0] = keys[:, cols]
        to_key[1] = values[:, cols]
        saved = attn_out[:, cols].astype(F32)
        centred = saved - jnp.mean(saved, axis=-1, keepdims=True)
        inverse = lax.rsqrt(jnp.mean(centred * centred, axis=-1, keepdims=True) + 1e-06)
        normed = centred * inverse
        gate_in = gate_pre[:, cols].astype(F32)
        grad_in = out_grad[:, cols].astype(F32)
        sigma = jax.nn.sigmoid(gate_in)
        gate_grad[:, cols] = (
            grad_in * normed * (sigma * (1.0 + gate_in * (1.0 - sigma)))
        ).astype(BF16)
        normed_grad = grad_in * (gate_in * sigma)
        to_query[1] = (
            inverse
            * (
                normed_grad
                - jnp.mean(normed_grad, axis=-1, keepdims=True)
                - normed * jnp.mean(normed_grad * normed, axis=-1, keepdims=True)
            )
        ).astype(BF16)


def prepare(queries, keys, values, attn_out, gate_pre, out_grad, after):
    rows, width = queries.shape
    step = min(rows // 2, 256)
    wide = pl.BlockSpec((step, width), lambda i: (i, 0))
    heads = lambda deep: pl.BlockSpec((deep, step, HEAD_DIM), lambda i: (0, i, 0))
    head_shape = lambda deep: jax.ShapeDtypeStruct((deep, rows, HEAD_DIM), BF16)
    return pl.pallas_call(
        prepare_kernel,
        grid=(rows // step,),
        in_specs=[wide] * 6 + [pl.BlockSpec(memory_space=pl.ANY)],
        out_specs=[heads(2), heads(2), heads(4), wide],
        out_shape=[
            head_shape(2),
            head_shape(2),
            head_shape(4),
            jax.ShapeDtypeStruct((rows, width), BF16),
        ],
        compiler_params=pltpu.CompilerParams(vmem_limit_bytes=VMEM_BYTES),
        cost_estimate=pl.CostEstimate(
            flops=40 * rows * width, bytes_accessed=22 * rows * width, transcendentals=rows * width
        ),
        name="prepare",
    )(queries, keys, values, attn_out, gate_pre, out_grad, after)


def attend_kernel(plan, first, last, ids, segs, seg_rows, *refs):
    blocks, refs = refs[: len(plan.blocks)], refs[len(plan.blocks) :]
    if not first:
        accs, refs = refs[:2], refs[2:]
    outs, (held, query_acc, key_acc, sems) = refs[:2], refs[2:]
    rows = held.shape[2]
    per = rows // TILE

    copies = [
        pltpu.make_async_copy(block, held.at[n], sems.at[n]) for n, block in enumerate(blocks)
    ]
    if first:
        query_acc[...] = jnp.zeros_like(query_acc)
        key_acc[...] = jnp.zeros_like(key_acc)
    else:
        copies += [
            pltpu.make_async_copy(source, target, sems.at[len(blocks) + n])
            for n, (source, target) in enumerate(zip(accs, (query_acc, key_acc)))
        ]
    for copy in copies:
        copy.start()
    waiting = set(range(len(copies)))

    def arrive(needed):
        for n in sorted(waiting & set(needed)):
            copies[n].wait()
            waiting.discard(n)

    arrive(range(len(blocks), len(copies)))

    def run(q_start, q_count, k_start, k_count, to_query, to_key):
        arrive(range(q_start, q_start + q_count))
        arrive(range(k_start, k_start + k_count))

        def pair_body(index, carry):
            q_blk, k_blk = index // k_count, index % k_count
            q_shard, k_shard = ids[q_start + q_blk], ids[k_start + k_blk]
            valid = (q_shard >= 0) & (k_shard >= 0) & (k_shard <= q_shard)
            q_shard, k_shard = jnp.maximum(q_shard, 0), jnp.maximum(k_shard, 0)
            meet = segs[k_shard * rows + rows - 1] >= segs[q_shard * rows]

            @pl.when(valid & meet)
            def _():
                lax.fori_loop(
                    0, per * per, functools.partial(tile_body, q_blk, k_blk, q_shard, k_shard), 0
                )

            return carry

        def tile_body(q_blk, k_blk, q_shard, k_shard, index, carry):
            q_off = pl.multiple_of((index // per) * TILE, TILE)
            k_off = pl.multiple_of((index % per) * TILE, TILE)
            q_held, k_held = q_start + q_blk, k_start + k_blk
            q_first, k_first = q_shard * rows + q_off, k_shard * rows + k_off
            q_last, k_last = q_first + TILE - 1, k_first + TILE - 1
            live = (k_first <= q_last) & (segs[k_last] >= segs[q_first])
            full = (k_last <= q_first) & (segs[k_first] == segs[q_last])
            q_rows, k_rows = pl.ds(q_off, TILE), pl.ds(k_off, TILE)

            def work(masked):
                query = held[q_held, 0, q_rows, :]
                grad = held[q_held, 1, q_rows, :]
                key = held[k_held, 0, k_rows, :]
                value = held[k_held, 1, k_rows, :]
                half = dot(key, query, ((1,), (1,))) * (SCALE / 2)
                slope_in = dot(value, grad, ((1,), (1,)))
                tanh = jnp.tanh(half)
                upper = 1.0 + tanh
                weights = half * upper
                score_grad = slope_in * (upper + weights * (1.0 - tanh))
                if masked:
                    seg_q = seg_rows[pl.ds(q_shard, 1), q_rows]
                    seg_k = seg_rows[pl.ds(k_shard, 1), k_rows]
                    seg_k = jnp.transpose(jnp.broadcast_to(seg_k, (HEAD_DIM, TILE)))[:, :1]
                    place_k = k_first + lax.broadcasted_iota(jnp.int32, (TILE, TILE), 0)
                    place_q = q_first + lax.broadcasted_iota(jnp.int32, (TILE, TILE), 1)
                    allowed = (seg_q == seg_k) & (place_k <= place_q)
                    weights = jnp.where(allowed, weights, 0.0)
                    score_grad = jnp.where(allowed, score_grad, 0.0)
                score_grad = score_grad.astype(BF16)
                if to_key:
                    weights = weights.astype(BF16)
                    key_acc[k_blk, 0, k_rows, :] += dot(score_grad, query, ((1,), (0,)))
                    key_acc[k_blk, 1, k_rows, :] += dot(weights, grad, ((1,), (0,)))
                if to_query:
                    query_acc[q_blk, q_rows, :] += dot(score_grad, key, ((0,), (0,)))

            @pl.when(live & full)
            def _():
                work(False)

            @pl.when(live & jnp.logical_not(full))
            def _():
                work(True)

            return carry

        lax.fori_loop(0, q_count * k_count, pair_body, 0)

    for entry in plan.entries:
        run(*entry)
    if last:
        for blk, out in enumerate(outs):
            out[0] = (query_acc[blk] * (SCALE / 2)).astype(BF16)
            out[1] = (key_acc[blk, 0] * (SCALE / 2)).astype(BF16)
            out[2] = key_acc[blk, 1].astype(BF16)
    else:
        done = [
            pltpu.make_async_copy(source, target, sems.at[n])
            for n, (source, target) in enumerate(zip((query_acc, key_acc), outs))
        ]
        for copy in done:
            copy.start()
        for copy in done:
            copy.wait()


class Plan:
    def __init__(self, shards):
        self.blocks, self.ids, self.entries = [], [], []
        self.shards = shards

    def add(self, blocks, ids):
        start = len(self.blocks)
        self.blocks += blocks
        self.ids += ids
        return start, len(blocks)


def attend(plan, first, last, segs, seg_rows, acc):
    rows = plan.blocks[0].shape[1]
    any_spec = pl.BlockSpec(memory_space=pl.ANY)
    vmem = pl.BlockSpec(memory_space=pltpu.VMEM)
    ids = jnp.stack(plan.ids).astype(jnp.int32)
    acc = [] if first else list(acc)
    query_shape, key_shape = (2, rows, HEAD_DIM), (2, 2, rows, HEAD_DIM)
    if last:
        out_shape = [jax.ShapeDtypeStruct((3, rows, HEAD_DIM), BF16)] * 2
    else:
        out_shape = [jax.ShapeDtypeStruct(query_shape, F32), jax.ShapeDtypeStruct(key_shape, F32)]
    return pl.pallas_call(
        functools.partial(attend_kernel, plan, first, last),
        grid_spec=pltpu.PrefetchScalarGridSpec(
            num_scalar_prefetch=2,
            grid=(),
            in_specs=[vmem] + [any_spec] * (len(plan.blocks) + len(acc)),
            out_specs=[vmem if last else any_spec] * 2,
            scratch_shapes=[
                pltpu.VMEM((len(plan.blocks), 2, rows, HEAD_DIM), BF16),
                pltpu.VMEM(query_shape, F32),
                pltpu.VMEM(key_shape, F32),
                pltpu.SemaphoreType.DMA((len(plan.blocks) + 2,)),
            ],
        ),
        out_shape=out_shape,
        compiler_params=pltpu.CompilerParams(vmem_limit_bytes=VMEM_BYTES),
        cost_estimate=pl.CostEstimate(
            flops=(1 if first else 2) * 2**7 * rows * rows * HEAD_DIM,
            bytes_accessed=16 * rows * HEAD_DIM * len(plan.blocks),
            transcendentals=4 * rows * rows,
        ),
        name="attend",
    )(ids, segs, seg_rows, *plan.blocks, *acc)


def project_early_kernel(place, own, gate_grad, weights, out):
    cols = pl.ds(pl.multiple_of(place[0] * HEAD_DIM, HEAD_DIM), HEAD_DIM)
    total = dot(gate_grad[...], weights[3], ((1,), (1,)))
    for part in range(3):
        total = total + dot(own[part], weights[part, :, cols], ((1,), (1,)))
    out[0] = total


def project_late_kernel(place, other, early, weights, out):
    cols = pl.ds(pl.multiple_of((1 - place[0]) * HEAD_DIM, HEAD_DIM), HEAD_DIM)
    total = early[0]
    for part in range(3):
        total = total + dot(other[part], weights[part, :, cols], ((1,), (1,)))
    out[0] = total.astype(out.dtype)


def project(place, skip, count, grads, early, projections, dtype):
    width = projections.shape[2]
    rows = grads[0].shape[-2]
    whole = lambda array: pl.BlockSpec(array.shape, lambda i, place: (0,) * array.ndim)
    partial = []
    if early is not None:
        partial = [pl.BlockSpec((1, rows, width), lambda i, place: (skip + i, 0, 0))]
    return pl.pallas_call(
        project_early_kernel if early is None else project_late_kernel,
        grid_spec=pltpu.PrefetchScalarGridSpec(
            num_scalar_prefetch=1,
            grid=(count,),
            in_specs=[whole(grad) for grad in grads]
            + partial
            + [pl.BlockSpec((4, width, width), lambda i, place: (0, place[1 + skip + i], 0))],
            out_specs=pl.BlockSpec((1, rows, width), lambda i, place: (i, 0, 0)),
        ),
        out_shape=jax.ShapeDtypeStruct((count, rows, width), dtype),
        compiler_params=pltpu.CompilerParams(vmem_limit_bytes=24 * 2**20),
        cost_estimate=pl.CostEstimate(
            flops=6 * count * rows * width * width,
            bytes_accessed=rows * width * (8 + 4 * count),
            transcendentals=0,
        ),
        name="project_early" if early is None else "project_late",
    )(place, *grads, *([] if early is None else [early]), projections)


def per_device(queries, key_rows, value_rows, attn_out, gate_pre, out_grad, segments, projections):
    rows = queries.shape[0]
    shards, groups = lax.axis_size("seq"), lax.axis_size("head")
    shard, group = lax.axis_index("seq"), lax.axis_index("head")
    pairs = shards // PAIR
    pair, lane = shard // PAIR, shard % PAIR

    def shift(block, distance, cross=0):
        route = [(i, (i + PAIR * distance) ^ cross) for i in range(shards)]
        return lax.ppermute(block, "seq", [hop for hop in route if 0 <= hop[1] < shards])

    seg_all = share(shards, segments.reshape(-1, HEAD_DIM))
    query_own, key_own, other, gate_grad = prepare(
        queries, key_rows, value_rows, attn_out, gate_pre, out_grad, seg_all
    )
    segs = seg_all.reshape(shards * rows)
    seg_rows = seg_all.reshape(shards, rows).astype(F32)
    reach = min((WINDOW + 1) // PAIR, pairs - 1)

    def travel(block, sign):
        arrived = {0: block}
        for distance in range(1, reach + 1):
            if distance == 2:
                arrived[distance] = shift(arrived[1], sign)
            else:
                arrived[distance] = shift(block, sign * distance)
        return arrived

    partner = shift(other, 0, 1)
    query_mine = [query_own, partner[:2]]
    key_mine = [key_own, partner[2:]]
    here = [shard, shard ^ 1]
    far_queries = [travel(block, -1) for block in query_mine]
    far_keys = [travel(block, 1) for block in key_mine]

    def far_ids(distance):
        far = pair + distance
        valid = (far >= 0) & (far < pairs)
        return [jnp.where(valid, PAIR * far + spot, -1) for spot in (lane, 1 - lane)]

    acc = None
    stages = [[0]] + [[distance] for distance in range(1, min(reach, 1) + 1)]
    if reach > 1:
        stages.append(list(range(2, reach + 1)))
    for number, stage in enumerate(stages):
        plan = Plan(shards)
        query_at = plan.add(query_mine, here)
        key_at = plan.add(key_mine, here)
        if number == 0:
            plan.entries.append((*query_at, *key_at, True, True))
        else:
            queries_in, keys_in, query_ids, key_ids = [], [], [], []
            for distance in stage:
                queries_in += [blocks[distance] for blocks in far_queries]
                keys_in += [blocks[distance] for blocks in far_keys]
                query_ids += far_ids(distance)
                key_ids += far_ids(-distance)
            plan.entries.append((*plan.add(queries_in, query_ids), *key_at, False, True))
            plan.entries.append((*query_at, *plan.add(keys_in, key_ids), True, False))
        acc = attend(plan, number == 0, number == len(stages) - 1, segs, seg_rows, acc)
    own_grads, other_grads = acc
    early = (own_grads, gate_grad)
    late = (shift(other_grads, 0, 1),)

    bits = []
    while (1 << len(bits)) < groups:
        bits.append(1 << len(bits))

    def across(block, bit):
        return lax.ppermute(block, "head", [(i, i ^ bit) for i in range(groups)])

    order = sorted(range(groups), key=lambda offset: (-(offset >> 1), -(offset & 1)))
    place = jnp.stack([lane] + [group ^ offset for offset in order]).astype(jnp.int32)
    base = project(place, 0, groups, early, None, projections, F32)
    sums = {}
    for number, offset in enumerate(order):
        if offset & 1:
            away = across(project(place, number, 1, late, base, projections, BF16)[0], 1)
        else:
            kept = project(place, number, 1, late, base, projections, F32)[0]
            sums[offset] = kept if groups == 1 else kept + away.astype(F32)
    for bit in reversed(bits[1:]):
        for offset in [held for held in sums if held & bit]:
            arrived = across(sums.pop(offset).astype(BF16), bit)
            sums[offset ^ bit] = sums[offset ^ bit] + arrived.astype(F32)
    return sums[0].astype(BF16)


def solution(mesh):
    return jax.shard_map(
        per_device,
        mesh=mesh,
        in_specs=(
            P("seq", "head"),
            P("seq", "head"),
            P("seq", "head"),
            P("seq", "head"),
            P("seq", "head"),
            P("seq", "head"),
            P("seq"),
            P(None, None, "head"),
        ),
        out_specs=P("seq", "head"),
        check_vma=False,
    )
```

```python
import functools

import jax
import jax.numpy as jnp
from jax import lax
from jax.experimental import pallas as pl
from jax.experimental.pallas import tpu as pltpu
from jax.sharding import PartitionSpec as P

HEAD_DIM = 128
WINDOW = 6
PAIR = 2
TILE = 512
SCALE = HEAD_DIM ** (-0.5)
VMEM_BYTES = 60 * 2**20
BF16 = jnp.bfloat16
F32 = jnp.float32


def dot(left, right, dims):
    return lax.dot_general(left, right, (dims, ((), ())), preferred_element_type=F32)


def prepare_kernel(
    shards, queries, keys, values, attn_out, gate_pre, out_grad, segments,
    query_own, key_own, other, gate_grad, seg_all, send_sems, recv_sems,
):
    me = lax.axis_index("seq")
    lane = lax.rem(me, PAIR)
    step = pl.program_id(0)

    def seg_copies():
        return [
            pltpu.make_async_remote_copy(
                src_ref=segments,
                dst_ref=seg_all.at[me],
                send_sem=send_sems.at[offset],
                recv_sem=recv_sems.at[offset],
                device_id={"seq": lax.rem(me + offset, shards)},
                device_id_type=pl.DeviceIdType.MESH,
            )
            for offset in range(1, shards)
        ]

    @pl.when(step == 0)
    def _():
        barrier = pltpu.get_barrier_semaphore()
        for offset in range(1, shards):
            pl.semaphore_signal(
                barrier,
                inc=1,
                device_id={"seq": lax.rem(me + offset, shards)},
                device_id_type=pl.DeviceIdType.MESH,
            )

    @pl.when(step == 1)
    def _():
        pl.semaphore_wait(pltpu.get_barrier_semaphore(), shards - 1)
        for copy in seg_copies():
            copy.start()
        own = pltpu.make_async_copy(segments, seg_all.at[me], send_sems.at[0])
        own.start()
        own.wait()

    for slot, (to_query, to_key) in enumerate(
        ((query_own, key_own), (other.at[pl.ds(0, 2)], other.at[pl.ds(2, 2)]))
    ):
        head = lane if slot == 0 else 1 - lane
        cols = pl.ds(pl.multiple_of(head * HEAD_DIM, HEAD_DIM), HEAD_DIM)
        to_query[0] = queries[:, cols]
        to_key[0] = keys[:, cols]
        to_key[1] = values[:, cols]
        saved = attn_out[:, cols].astype(F32)
        centred = saved - jnp.mean(saved, axis=-1, keepdims=True)
        inverse = lax.rsqrt(jnp.mean(centred * centred, axis=-1, keepdims=True) + 1e-06)
        normed = centred * inverse
        gate_in = gate_pre[:, cols].astype(F32)
        grad_in = out_grad[:, cols].astype(F32)
        sigma = jax.nn.sigmoid(gate_in)
        gate_grad[:, cols] = (
            grad_in * normed * (sigma * (1.0 + gate_in * (1.0 - sigma)))
        ).astype(BF16)
        normed_grad = grad_in * (gate_in * sigma)
        to_query[1] = (
            inverse
            * (
                normed_grad
                - jnp.mean(normed_grad, axis=-1, keepdims=True)
                - normed * jnp.mean(normed_grad * normed, axis=-1, keepdims=True)
            )
        ).astype(BF16)

    @pl.when(step == pl.num_programs(0) - 1)
    def _():
        for copy in seg_copies():
            copy.wait()


def prepare(shards, queries, keys, values, attn_out, gate_pre, out_grad, segments):
    rows, width = queries.shape
    step = min(rows // 2, 256)
    wide = pl.BlockSpec((step, width), lambda i: (i, 0))
    heads = lambda deep: pl.BlockSpec((deep, step, HEAD_DIM), lambda i: (0, i, 0))
    head_shape = lambda deep: jax.ShapeDtypeStruct((deep, rows, HEAD_DIM), BF16)
    return pl.pallas_call(
        functools.partial(prepare_kernel, shards),
        grid=(rows // step,),
        in_specs=[wide] * 6 + [pl.BlockSpec(memory_space=pl.ANY)],
        out_specs=[heads(2), heads(2), heads(4), wide, pl.BlockSpec(memory_space=pl.ANY)],
        out_shape=[
            head_shape(2),
            head_shape(2),
            head_shape(4),
            jax.ShapeDtypeStruct((rows, width), BF16),
            jax.ShapeDtypeStruct((shards,) + segments.shape, segments.dtype),
        ],
        scratch_shapes=[
            pltpu.SemaphoreType.DMA((shards,)),
            pltpu.SemaphoreType.DMA((shards,)),
        ],
        compiler_params=pltpu.CompilerParams(
            vmem_limit_bytes=VMEM_BYTES, collective_id=0, has_side_effects=True
        ),
        cost_estimate=pl.CostEstimate(
            flops=40 * rows * width, bytes_accessed=22 * rows * width, transcendentals=rows * width
        ),
        name="prepare",
    )(queries, keys, values, attn_out, gate_pre, out_grad, segments)


def attend_kernel(plan, first, last, ids, segs, seg_rows, *refs):
    blocks, refs = refs[: len(plan.blocks)], refs[len(plan.blocks) :]
    if not first:
        accs, refs = refs[:2], refs[2:]
    outs, (held, query_acc, key_acc, sems) = refs[:2], refs[2:]
    rows = held.shape[2]
    per = rows // TILE

    copies = [
        pltpu.make_async_copy(block, held.at[n], sems.at[n]) for n, block in enumerate(blocks)
    ]
    if first:
        query_acc[...] = jnp.zeros_like(query_acc)
        key_acc[...] = jnp.zeros_like(key_acc)
    else:
        copies += [
            pltpu.make_async_copy(source, target, sems.at[len(blocks) + n])
            for n, (source, target) in enumerate(zip(accs, (query_acc, key_acc)))
        ]
    for copy in copies:
        copy.start()
    waiting = set(range(len(copies)))

    def arrive(needed):
        for n in sorted(waiting & set(needed)):
            copies[n].wait()
            waiting.discard(n)

    arrive(range(len(blocks), len(copies)))

    def run(q_start, q_count, k_start, k_count, to_query, to_key):
        arrive(range(q_start, q_start + q_count))
        arrive(range(k_start, k_start + k_count))

        def pair_body(index, carry):
            q_blk, k_blk = index // k_count, index % k_count
            q_shard, k_shard = ids[q_start + q_blk], ids[k_start + k_blk]
            valid = (q_shard >= 0) & (k_shard >= 0) & (k_shard <= q_shard)
            q_shard, k_shard = jnp.maximum(q_shard, 0), jnp.maximum(k_shard, 0)
            meet = segs[k_shard * rows + rows - 1] >= segs[q_shard * rows]

            @pl.when(valid & meet)
            def _():
                lax.fori_loop(
                    0, per * per, functools.partial(tile_body, q_blk, k_blk, q_shard, k_shard), 0
                )

            return carry

        def tile_body(q_blk, k_blk, q_shard, k_shard, index, carry):
            q_off = pl.multiple_of((index // per) * TILE, TILE)
            k_off = pl.multiple_of((index % per) * TILE, TILE)
            q_held, k_held = q_start + q_blk, k_start + k_blk
            q_first, k_first = q_shard * rows + q_off, k_shard * rows + k_off
            q_last, k_last = q_first + TILE - 1, k_first + TILE - 1
            live = (k_first <= q_last) & (segs[k_last] >= segs[q_first])
            full = (k_last <= q_first) & (segs[k_first] == segs[q_last])
            q_rows, k_rows = pl.ds(q_off, TILE), pl.ds(k_off, TILE)

            def work(masked):
                query = held[q_held, 0, q_rows, :]
                grad = held[q_held, 1, q_rows, :]
                key = held[k_held, 0, k_rows, :]
                value = held[k_held, 1, k_rows, :]
                half = dot(key, query, ((1,), (1,))) * (SCALE / 2)
                slope_in = dot(value, grad, ((1,), (1,)))
                tanh = jnp.tanh(half)
                upper = 1.0 + tanh
                weights = half * upper
                score_grad = slope_in * (upper + weights * (1.0 - tanh))
                if masked:
                    seg_q = seg_rows[pl.ds(q_shard, 1), q_rows]
                    seg_k = seg_rows[pl.ds(k_shard, 1), k_rows]
                    seg_k = jnp.transpose(jnp.broadcast_to(seg_k, (HEAD_DIM, TILE)))[:, :1]
                    place_k = k_first + lax.broadcasted_iota(jnp.int32, (TILE, TILE), 0)
                    place_q = q_first + lax.broadcasted_iota(jnp.int32, (TILE, TILE), 1)
                    allowed = (seg_q == seg_k) & (place_k <= place_q)
                    weights = jnp.where(allowed, weights, 0.0)
                    score_grad = jnp.where(allowed, score_grad, 0.0)
                score_grad = score_grad.astype(BF16)
                if to_key:
                    weights = weights.astype(BF16)
                    key_acc[k_blk, 0, k_rows, :] += dot(score_grad, query, ((1,), (0,)))
                    key_acc[k_blk, 1, k_rows, :] += dot(weights, grad, ((1,), (0,)))
                if to_query:
                    query_acc[q_blk, q_rows, :] += dot(score_grad, key, ((0,), (0,)))

            @pl.when(live & full)
            def _():
                work(False)

            @pl.when(live & jnp.logical_not(full))
            def _():
                work(True)

            return carry

        lax.fori_loop(0, q_count * k_count, pair_body, 0)

    for entry in plan.entries:
        run(*entry)
    if last:
        for blk, out in enumerate(outs):
            out[0] = (query_acc[blk] * (SCALE / 2)).astype(BF16)
            out[1] = (key_acc[blk, 0] * (SCALE / 2)).astype(BF16)
            out[2] = key_acc[blk, 1].astype(BF16)
    else:
        done = [
            pltpu.make_async_copy(source, target, sems.at[n])
            for n, (source, target) in enumerate(zip((query_acc, key_acc), outs))
        ]
        for copy in done:
            copy.start()
        for copy in done:
            copy.wait()


class Plan:
    def __init__(self, shards):
        self.blocks, self.ids, self.entries = [], [], []
        self.shards = shards

    def add(self, blocks, ids):
        start = len(self.blocks)
        self.blocks += blocks
        self.ids += ids
        return start, len(blocks)


def attend(plan, first, last, segs, seg_rows, acc):
    rows = plan.blocks[0].shape[1]
    any_spec = pl.BlockSpec(memory_space=pl.ANY)
    vmem = pl.BlockSpec(memory_space=pltpu.VMEM)
    ids = jnp.stack(plan.ids).astype(jnp.int32)
    acc = [] if first else list(acc)
    query_shape, key_shape = (2, rows, HEAD_DIM), (2, 2, rows, HEAD_DIM)
    if last:
        out_shape = [jax.ShapeDtypeStruct((3, rows, HEAD_DIM), BF16)] * 2
    else:
        out_shape = [jax.ShapeDtypeStruct(query_shape, F32), jax.ShapeDtypeStruct(key_shape, F32)]
    return pl.pallas_call(
        functools.partial(attend_kernel, plan, first, last),
        grid_spec=pltpu.PrefetchScalarGridSpec(
            num_scalar_prefetch=2,
            grid=(),
            in_specs=[vmem] + [any_spec] * (len(plan.blocks) + len(acc)),
            out_specs=[vmem if last else any_spec] * 2,
            scratch_shapes=[
                pltpu.VMEM((len(plan.blocks), 2, rows, HEAD_DIM), BF16),
                pltpu.VMEM(query_shape, F32),
                pltpu.VMEM(key_shape, F32),
                pltpu.SemaphoreType.DMA((len(plan.blocks) + 2,)),
            ],
        ),
        out_shape=out_shape,
        compiler_params=pltpu.CompilerParams(vmem_limit_bytes=24 * 2**20),
        cost_estimate=pl.CostEstimate(
            flops=(1 if first else 2) * 2**7 * rows * rows * HEAD_DIM,
            bytes_accessed=16 * rows * HEAD_DIM * len(plan.blocks),
            transcendentals=4 * rows * rows,
        ),
        name="attend",
    )(ids, segs, seg_rows, *plan.blocks, *acc)


def project_early_kernel(place, own, gate_grad, weights, out):
    cols = pl.ds(pl.multiple_of(place[0] * HEAD_DIM, HEAD_DIM), HEAD_DIM)
    total = dot(gate_grad[...], weights[3], ((1,), (1,)))
    for part in range(3):
        total = total + dot(own[part], weights[part, :, cols], ((1,), (1,)))
    out[0] = total


def project_late_kernel(place, other, early, weights, out):
    cols = pl.ds(pl.multiple_of((1 - place[0]) * HEAD_DIM, HEAD_DIM), HEAD_DIM)
    total = early[0]
    for part in range(3):
        total = total + dot(other[part], weights[part, :, cols], ((1,), (1,)))
    out[0] = total.astype(out.dtype)


def project(place, skip, count, grads, early, projections, dtype):
    width = projections.shape[2]
    rows = grads[0].shape[-2]
    whole = lambda array: pl.BlockSpec(array.shape, lambda i, place: (0,) * array.ndim)
    partial = []
    if early is not None:
        partial = [pl.BlockSpec((1, rows, width), lambda i, place: (skip + i, 0, 0))]
    return pl.pallas_call(
        project_early_kernel if early is None else project_late_kernel,
        grid_spec=pltpu.PrefetchScalarGridSpec(
            num_scalar_prefetch=1,
            grid=(count,),
            in_specs=[whole(grad) for grad in grads]
            + partial
            + [pl.BlockSpec((4, width, width), lambda i, place: (0, place[1 + skip + i], 0))],
            out_specs=pl.BlockSpec((1, rows, width), lambda i, place: (i, 0, 0)),
        ),
        out_shape=jax.ShapeDtypeStruct((count, rows, width), dtype),
        compiler_params=pltpu.CompilerParams(vmem_limit_bytes=24 * 2**20),
        cost_estimate=pl.CostEstimate(
            flops=6 * count * rows * width * width,
            bytes_accessed=rows * width * (8 + 4 * count),
            transcendentals=0,
        ),
        name="project_early" if early is None else "project_late",
    )(place, *grads, *([] if early is None else [early]), projections)


def per_device(queries, key_rows, value_rows, attn_out, gate_pre, out_grad, segments, projections):
    rows = queries.shape[0]
    shards, groups = lax.axis_size("seq"), lax.axis_size("head")
    shard, group = lax.axis_index("seq"), lax.axis_index("head")
    pairs = shards // PAIR
    pair, lane = shard // PAIR, shard % PAIR

    def shift(block, distance, cross=0):
        route = [(i, (i + PAIR * distance) ^ cross) for i in range(shards)]
        return lax.ppermute(block, "seq", [hop for hop in route if 0 <= hop[1] < shards])

    query_own, key_own, other, gate_grad, seg_all = prepare(
        shards, queries, key_rows, value_rows, attn_out, gate_pre, out_grad,
        segments.reshape(-1, HEAD_DIM),
    )
    segs = seg_all.reshape(shards * rows)
    seg_rows = seg_all.reshape(shards, rows).astype(F32)
    reach = min((WINDOW + 1) // PAIR, pairs - 1)

    def travel(block, sign):
        arrived = {0: block}
        for distance in range(1, reach + 1):
            if distance == 2:
                arrived[distance] = shift(arrived[1], sign)
            else:
                arrived[distance] = shift(block, sign * distance)
        return arrived

    partner = shift(other, 0, 1)
    query_mine = [query_own, partner[:2]]
    key_mine = [key_own, partner[2:]]
    here = [shard, shard ^ 1]
    far_queries = [travel(block, -1) for block in query_mine]
    far_keys = [travel(block, 1) for block in key_mine]

    def far_ids(distance):
        far = pair + distance
        valid = (far >= 0) & (far < pairs)
        return [jnp.where(valid, PAIR * far + spot, -1) for spot in (lane, 1 - lane)]

    acc = None
    stages = [[0]] + [[distance] for distance in range(1, min(reach, 1) + 1)]
    if reach > 1:
        stages.append(list(range(2, reach + 1)))
    for number, stage in enumerate(stages):
        plan = Plan(shards)
        query_at = plan.add(query_mine, here)
        key_at = plan.add(key_mine, here)
        if number == 0:
            plan.entries.append((*query_at, *key_at, True, True))
        else:
            queries_in, keys_in, query_ids, key_ids = [], [], [], []
            for distance in stage:
                queries_in += [blocks[distance] for blocks in far_queries]
                keys_in += [blocks[distance] for blocks in far_keys]
                query_ids += far_ids(distance)
                key_ids += far_ids(-distance)
            plan.entries.append((*plan.add(queries_in, query_ids), *key_at, False, True))
            plan.entries.append((*query_at, *plan.add(keys_in, key_ids), True, False))
        acc = attend(plan, number == 0, number == len(stages) - 1, segs, seg_rows, acc)
    own_grads, other_grads = acc
    early = (own_grads, gate_grad)
    late = (shift(other_grads, 0, 1),)

    bits = []
    while (1 << len(bits)) < groups:
        bits.append(1 << len(bits))

    def across(block, bit):
        return lax.ppermute(block, "head", [(i, i ^ bit) for i in range(groups)])

    order = sorted(range(groups), key=lambda offset: (-(offset >> 1), -(offset & 1)))
    place = jnp.stack([lane] + [group ^ offset for offset in order]).astype(jnp.int32)
    base = project(place, 0, groups, early, None, projections, F32)
    sums = {}
    for number, offset in enumerate(order):
        if offset & 1:
            away = across(project(place, number, 1, late, base, projections, BF16)[0], 1)
        else:
            kept = project(place, number, 1, late, base, projections, F32)[0]
            sums[offset] = kept if groups == 1 else kept + away.astype(F32)
    for bit in reversed(bits[1:]):
        for offset in [held for held in sums if held & bit]:
            arrived = across(sums.pop(offset).astype(BF16), bit)
            sums[offset ^ bit] = sums[offset ^ bit] + arrived.astype(F32)
    return sums[0].astype(BF16)


def solution(mesh):
    return jax.shard_map(
        per_device,
        mesh=mesh,
        in_specs=(
            P("seq", "head"),
            P("seq", "head"),
            P("seq", "head"),
            P("seq", "head"),
            P("seq", "head"),
            P("seq", "head"),
            P("seq"),
            P(None, None, "head"),
        ),
        out_specs=P("seq", "head"),
        check_vma=False,
    )
```

```python
import functools

import jax
import jax.numpy as jnp
from jax import lax
from jax.experimental import pallas as pl
from jax.experimental.pallas import tpu as pltpu
from jax.sharding import PartitionSpec as P

HEAD_DIM = 128
WINDOW = 6
PAIR = 2
TILE = 512
SCALE = HEAD_DIM ** (-0.5)
VMEM_BYTES = 60 * 2**20
BF16 = jnp.bfloat16
F32 = jnp.float32


def dot(left, right, dims):
    return lax.dot_general(left, right, (dims, ((), ())), preferred_element_type=F32)


def prepare_kernel(
    shards, queries, keys, values, attn_out, gate_pre, out_grad, segments,
    query_own, key_own, query_other, key_other, gate_grad, seg_all, send_sems, recv_sems,
):
    me = lax.axis_index("seq")
    lane = lax.rem(me, PAIR)
    step = pl.program_id(0)

    def seg_copies():
        return [
            pltpu.make_async_remote_copy(
                src_ref=segments,
                dst_ref=seg_all.at[me],
                send_sem=send_sems.at[offset],
                recv_sem=recv_sems.at[offset],
                device_id={"seq": lax.rem(me + offset, shards)},
                device_id_type=pl.DeviceIdType.MESH,
            )
            for offset in range(1, shards)
        ]

    @pl.when(step == 0)
    def _():
        barrier = pltpu.get_barrier_semaphore()
        for offset in range(1, shards):
            pl.semaphore_signal(
                barrier,
                inc=1,
                device_id={"seq": lax.rem(me + offset, shards)},
                device_id_type=pl.DeviceIdType.MESH,
            )

    @pl.when(step == 1)
    def _():
        pl.semaphore_wait(pltpu.get_barrier_semaphore(), shards - 1)
        for copy in seg_copies():
            copy.start()
        own = pltpu.make_async_copy(segments, seg_all.at[me], send_sems.at[0])
        own.start()
        own.wait()

    for slot, (to_query, to_key) in enumerate(
        ((query_own, key_own), (query_other, key_other))
    ):
        head = lane if slot == 0 else 1 - lane
        cols = pl.ds(pl.multiple_of(head * HEAD_DIM, HEAD_DIM), HEAD_DIM)
        to_query[0] = queries[:, cols]
        to_key[0] = keys[:, cols]
        to_key[1] = values[:, cols]
        saved = attn_out[:, cols].astype(F32)
        centred = saved - jnp.mean(saved, axis=-1, keepdims=True)
        inverse = lax.rsqrt(jnp.mean(centred * centred, axis=-1, keepdims=True) + 1e-06)
        normed = centred * inverse
        gate_in = gate_pre[:, cols].astype(F32)
        grad_in = out_grad[:, cols].astype(F32)
        sigma = jax.nn.sigmoid(gate_in)
        gate_grad[:, cols] = (
            grad_in * normed * (sigma * (1.0 + gate_in * (1.0 - sigma)))
        ).astype(BF16)
        normed_grad = grad_in * (gate_in * sigma)
        to_query[1] = (
            inverse
            * (
                normed_grad
                - jnp.mean(normed_grad, axis=-1, keepdims=True)
                - normed * jnp.mean(normed_grad * normed, axis=-1, keepdims=True)
            )
        ).astype(BF16)

    @pl.when(step == pl.num_programs(0) - 1)
    def _():
        for copy in seg_copies():
            copy.wait()


def prepare(shards, queries, keys, values, attn_out, gate_pre, out_grad, segments):
    rows, width = queries.shape
    step = min(rows // 2, 256)
    wide = pl.BlockSpec((step, width), lambda i: (i, 0))
    heads = lambda deep: pl.BlockSpec((deep, step, HEAD_DIM), lambda i: (0, i, 0))
    head_shape = lambda deep: jax.ShapeDtypeStruct((deep, rows, HEAD_DIM), BF16)
    return pl.pallas_call(
        functools.partial(prepare_kernel, shards),
        grid=(rows // step,),
        in_specs=[wide] * 6 + [pl.BlockSpec(memory_space=pl.ANY)],
        out_specs=[heads(2), heads(2), heads(2), heads(2), wide, pl.BlockSpec(memory_space=pl.ANY)],
        out_shape=[
            head_shape(2),
            head_shape(2),
            head_shape(2),
            head_shape(2),
            jax.ShapeDtypeStruct((rows, width), BF16),
            jax.ShapeDtypeStruct((shards,) + segments.shape, segments.dtype),
        ],
        scratch_shapes=[
            pltpu.SemaphoreType.DMA((shards,)),
            pltpu.SemaphoreType.DMA((shards,)),
        ],
        compiler_params=pltpu.CompilerParams(
            vmem_limit_bytes=VMEM_BYTES, collective_id=0, has_side_effects=True
        ),
        cost_estimate=pl.CostEstimate(
            flops=40 * rows * width, bytes_accessed=22 * rows * width, transcendentals=rows * width
        ),
        name="prepare",
    )(queries, keys, values, attn_out, gate_pre, out_grad, segments)


def attend_kernel(plan, first, last, ids, segs, seg_rows, *refs):
    blocks, refs = refs[: len(plan.blocks)], refs[len(plan.blocks) :]
    if not first:
        accs, refs = refs[:2], refs[2:]
    outs, (held, query_acc, key_acc, sems) = refs[:2], refs[2:]
    rows = held.shape[2]
    per = rows // TILE

    copies = [
        pltpu.make_async_copy(block, held.at[n], sems.at[n]) for n, block in enumerate(blocks)
    ]
    if first:
        query_acc[...] = jnp.zeros_like(query_acc)
        key_acc[...] = jnp.zeros_like(key_acc)
    else:
        copies += [
            pltpu.make_async_copy(source, target, sems.at[len(blocks) + n])
            for n, (source, target) in enumerate(zip(accs, (query_acc, key_acc)))
        ]
    for copy in copies:
        copy.start()
    waiting = set(range(len(copies)))

    def arrive(needed):
        for n in sorted(waiting & set(needed)):
            copies[n].wait()
            waiting.discard(n)

    arrive(range(len(blocks), len(copies)))

    def run(q_start, q_count, k_start, k_count, to_query, to_key):
        arrive(range(q_start, q_start + q_count))
        arrive(range(k_start, k_start + k_count))

        def pair_body(index, carry):
            q_blk, k_blk = index // k_count, index % k_count
            q_shard, k_shard = ids[q_start + q_blk], ids[k_start + k_blk]
            valid = (q_shard >= 0) & (k_shard >= 0) & (k_shard <= q_shard)
            q_shard, k_shard = jnp.maximum(q_shard, 0), jnp.maximum(k_shard, 0)
            meet = segs[k_shard * rows + rows - 1] >= segs[q_shard * rows]

            @pl.when(valid & meet)
            def _():
                lax.fori_loop(
                    0, per * per, functools.partial(tile_body, q_blk, k_blk, q_shard, k_shard), 0
                )

            return carry

        def tile_body(q_blk, k_blk, q_shard, k_shard, index, carry):
            q_off = pl.multiple_of((index // per) * TILE, TILE)
            k_off = pl.multiple_of((index % per) * TILE, TILE)
            q_held, k_held = q_start + q_blk, k_start + k_blk
            q_first, k_first = q_shard * rows + q_off, k_shard * rows + k_off
            q_last, k_last = q_first + TILE - 1, k_first + TILE - 1
            live = (k_first <= q_last) & (segs[k_last] >= segs[q_first])
            full = (k_last <= q_first) & (segs[k_first] == segs[q_last])
            q_rows, k_rows = pl.ds(q_off, TILE), pl.ds(k_off, TILE)

            def work(masked):
                query = held[q_held, 0, q_rows, :]
                grad = held[q_held, 1, q_rows, :]
                key = held[k_held, 0, k_rows, :]
                value = held[k_held, 1, k_rows, :]
                half = dot(key, query, ((1,), (1,))) * (SCALE / 2)
                slope_in = dot(value, grad, ((1,), (1,)))
                tanh = jnp.tanh(half)
                upper = 1.0 + tanh
                weights = half * upper
                score_grad = slope_in * (upper + weights * (1.0 - tanh))
                if masked:
                    seg_q = seg_rows[pl.ds(q_shard, 1), q_rows]
                    seg_k = seg_rows[pl.ds(k_shard, 1), k_rows]
                    seg_k = jnp.transpose(jnp.broadcast_to(seg_k, (HEAD_DIM, TILE)))[:, :1]
                    place_k = k_first + lax.broadcasted_iota(jnp.int32, (TILE, TILE), 0)
                    place_q = q_first + lax.broadcasted_iota(jnp.int32, (TILE, TILE), 1)
                    allowed = (seg_q == seg_k) & (place_k <= place_q)
                    weights = jnp.where(allowed, weights, 0.0)
                    score_grad = jnp.where(allowed, score_grad, 0.0)
                score_grad = score_grad.astype(BF16)
                if to_key:
                    weights = weights.astype(BF16)
                    key_acc[k_blk, 0, k_rows, :] += dot(score_grad, query, ((1,), (0,)))
                    key_acc[k_blk, 1, k_rows, :] += dot(weights, grad, ((1,), (0,)))
                if to_query:
                    query_acc[q_blk, q_rows, :] += dot(score_grad, key, ((0,), (0,)))

            @pl.when(live & full)
            def _():
                work(False)

            @pl.when(live & jnp.logical_not(full))
            def _():
                work(True)

            return carry

        lax.fori_loop(0, q_count * k_count, pair_body, 0)

    for entry in plan.entries:
        run(*entry)
    if last:
        for blk, out in enumerate(outs):
            out[0] = (query_acc[blk] * (SCALE / 2)).astype(BF16)
            out[1] = (key_acc[blk, 0] * (SCALE / 2)).astype(BF16)
            out[2] = key_acc[blk, 1].astype(BF16)
    else:
        done = [
            pltpu.make_async_copy(source, target, sems.at[n])
            for n, (source, target) in enumerate(zip((query_acc, key_acc), outs))
        ]
        for copy in done:
            copy.start()
        for copy in done:
            copy.wait()


class Plan:
    def __init__(self, shards):
        self.blocks, self.ids, self.entries = [], [], []
        self.shards = shards

    def add(self, blocks, ids):
        start = len(self.blocks)
        self.blocks += blocks
        self.ids += ids
        return start, len(blocks)


def attend(plan, first, last, segs, seg_rows, acc):
    rows = plan.blocks[0].shape[1]
    any_spec = pl.BlockSpec(memory_space=pl.ANY)
    vmem = pl.BlockSpec(memory_space=pltpu.VMEM)
    ids = jnp.stack(plan.ids).astype(jnp.int32)
    acc = [] if first else list(acc)
    query_shape, key_shape = (2, rows, HEAD_DIM), (2, 2, rows, HEAD_DIM)
    if last:
        out_shape = [jax.ShapeDtypeStruct((3, rows, HEAD_DIM), BF16)] * 2
    else:
        out_shape = [jax.ShapeDtypeStruct(query_shape, F32), jax.ShapeDtypeStruct(key_shape, F32)]
    return pl.pallas_call(
        functools.partial(attend_kernel, plan, first, last),
        grid_spec=pltpu.PrefetchScalarGridSpec(
            num_scalar_prefetch=2,
            grid=(),
            in_specs=[vmem] + [any_spec] * (len(plan.blocks) + len(acc)),
            out_specs=[vmem if last else any_spec] * 2,
            scratch_shapes=[
                pltpu.VMEM((len(plan.blocks), 2, rows, HEAD_DIM), BF16),
                pltpu.VMEM(query_shape, F32),
                pltpu.VMEM(key_shape, F32),
                pltpu.SemaphoreType.DMA((len(plan.blocks) + 2,)),
            ],
        ),
        out_shape=out_shape,
        compiler_params=pltpu.CompilerParams(vmem_limit_bytes=24 * 2**20),
        cost_estimate=pl.CostEstimate(
            flops=(1 if first else 2) * 2**7 * rows * rows * HEAD_DIM,
            bytes_accessed=16 * rows * HEAD_DIM * len(plan.blocks),
            transcendentals=4 * rows * rows,
        ),
        name="attend",
    )(ids, segs, seg_rows, *plan.blocks, *acc)


def project_early_kernel(place, own, gate_grad, weights, out):
    cols = pl.ds(pl.multiple_of(place[0] * HEAD_DIM, HEAD_DIM), HEAD_DIM)
    total = dot(gate_grad[...], weights[3], ((1,), (1,)))
    for part in range(3):
        total = total + dot(own[part], weights[part, :, cols], ((1,), (1,)))
    out[0] = total


def project_late_kernel(place, other, early, weights, out):
    cols = pl.ds(pl.multiple_of((1 - place[0]) * HEAD_DIM, HEAD_DIM), HEAD_DIM)
    total = early[0]
    for part in range(3):
        total = total + dot(other[part], weights[part, :, cols], ((1,), (1,)))
    out[0] = total.astype(out.dtype)


def project(place, skip, count, grads, early, projections, dtype):
    width = projections.shape[2]
    rows = grads[0].shape[-2]
    whole = lambda array: pl.BlockSpec(array.shape, lambda i, place: (0,) * array.ndim)
    partial = []
    if early is not None:
        partial = [pl.BlockSpec((1, rows, width), lambda i, place: (skip + i, 0, 0))]
    return pl.pallas_call(
        project_early_kernel if early is None else project_late_kernel,
        grid_spec=pltpu.PrefetchScalarGridSpec(
            num_scalar_prefetch=1,
            grid=(count,),
            in_specs=[whole(grad) for grad in grads]
            + partial
            + [pl.BlockSpec((4, width, width), lambda i, place: (0, place[1 + skip + i], 0))],
            out_specs=pl.BlockSpec((1, rows, width), lambda i, place: (i, 0, 0)),
        ),
        out_shape=jax.ShapeDtypeStruct((count, rows, width), dtype),
        compiler_params=pltpu.CompilerParams(vmem_limit_bytes=24 * 2**20),
        cost_estimate=pl.CostEstimate(
            flops=6 * count * rows * width * width,
            bytes_accessed=rows * width * (8 + 4 * count),
            transcendentals=0,
        ),
        name="project_early" if early is None else "project_late",
    )(place, *grads, *([] if early is None else [early]), projections)


def per_device(queries, key_rows, value_rows, attn_out, gate_pre, out_grad, segments, projections):
    rows = queries.shape[0]
    shards, groups = lax.axis_size("seq"), lax.axis_size("head")
    shard, group = lax.axis_index("seq"), lax.axis_index("head")
    pairs = shards // PAIR
    pair, lane = shard // PAIR, shard % PAIR

    def shift(block, distance, cross=0):
        route = [(i, (i + PAIR * distance) ^ cross) for i in range(shards)]
        return lax.ppermute(block, "seq", [hop for hop in route if 0 <= hop[1] < shards])

    query_own, key_own, query_other, key_other, gate_grad, seg_all = prepare(
        shards, queries, key_rows, value_rows, attn_out, gate_pre, out_grad,
        segments.reshape(-1, HEAD_DIM),
    )
    segs = seg_all.reshape(shards * rows)
    seg_rows = seg_all.reshape(shards, rows).astype(F32)
    reach = min((WINDOW + 1) // PAIR, pairs - 1)

    def travel(block, sign):
        arrived = {0: block}
        for distance in range(1, reach + 1):
            if distance == 2:
                arrived[distance] = shift(arrived[1], sign)
            else:
                arrived[distance] = shift(block, sign * distance)
        return arrived

    query_mine = [query_own, shift(query_other, 0, 1)]
    key_mine = [key_own, shift(key_other, 0, 1)]
    here = [shard, shard ^ 1]
    far_queries = [travel(block, -1) for block in query_mine]
    far_keys = [travel(block, 1) for block in key_mine]

    def far_ids(distance):
        far = pair + distance
        valid = (far >= 0) & (far < pairs)
        return [jnp.where(valid, PAIR * far + spot, -1) for spot in (lane, 1 - lane)]

    acc = None
    stages = [[0]] + [[distance] for distance in range(1, min(reach, 1) + 1)]
    if reach > 1:
        stages.append(list(range(2, reach + 1)))
    for number, stage in enumerate(stages):
        plan = Plan(shards)
        query_at = plan.add(query_mine, here)
        key_at = plan.add(key_mine, here)
        if number == 0:
            plan.entries.append((*query_at, *key_at, True, True))
        else:
            queries_in, keys_in, query_ids, key_ids = [], [], [], []
            for distance in stage:
                queries_in += [blocks[distance] for blocks in far_queries]
                keys_in += [blocks[distance] for blocks in far_keys]
                query_ids += far_ids(distance)
                key_ids += far_ids(-distance)
            plan.entries.append((*plan.add(queries_in, query_ids), *key_at, False, True))
            plan.entries.append((*query_at, *plan.add(keys_in, key_ids), True, False))
        acc = attend(plan, number == 0, number == len(stages) - 1, segs, seg_rows, acc)
    own_grads, other_grads = acc
    early = (own_grads, gate_grad)
    late = (shift(other_grads, 0, 1),)

    bits = []
    while (1 << len(bits)) < groups:
        bits.append(1 << len(bits))

    def across(block, bit):
        return lax.ppermute(block, "head", [(i, i ^ bit) for i in range(groups)])

    order = sorted(range(groups), key=lambda offset: (-(offset >> 1), -(offset & 1)))
    place = jnp.stack([lane] + [group ^ offset for offset in order]).astype(jnp.int32)
    base = project(place, 0, groups, early, None, projections, F32)
    sums = {}
    for number, offset in enumerate(order):
        if offset & 1:
            away = across(project(place, number, 1, late, base, projections, BF16)[0], 1)
        else:
            kept = project(place, number, 1, late, base, projections, F32)[0]
            sums[offset] = kept if groups == 1 else kept + away.astype(F32)
    for bit in reversed(bits[1:]):
        for offset in [held for held in sums if held & bit]:
            arrived = across(sums.pop(offset).astype(BF16), bit)
            sums[offset ^ bit] = sums[offset ^ bit] + arrived.astype(F32)
    return sums[0].astype(BF16)


def solution(mesh):
    return jax.shard_map(
        per_device,
        mesh=mesh,
        in_specs=(
            P("seq", "head"),
            P("seq", "head"),
            P("seq", "head"),
            P("seq", "head"),
            P("seq", "head"),
            P("seq", "head"),
            P("seq"),
            P(None, None, "head"),
        ),
        out_specs=P("seq", "head"),
        check_vma=False,
    )
```
